128 devices in a mesh: slab: 4 (over z_lo, core), dev: 32 (over y, z_hi, x).
Axes of the slice: x: 4, y: 4, z: 4 (z_hi: 2, z_lo: 2; z = z_hi * 2 + z_lo), core: 2. Of those that a mesh axis runs over, the one named last changes fastest.
Arguments:
- tilts: bfloat16 [32, 384, 3072], P('dev', 'slab'), may hold values from -6 to 6
- tilt_defocus: float32 [32], P('dev'), may hold values from 1 to 3
- defocus_table: float32 [8], replicated, may hold values from 0.2 to 1
- slab_pick: int32 [4], P('slab'), may hold values from 0 to 7
- interp_offset: int32 [32, 16], P(None, 'slab'), may hold values from -768 to 768
- interp_weights: bfloat16 [32, 16, 4], P(None, 'slab'), may hold values from -0.5 to 0.5
Outputs:
- volume: float32 [384, 16, 3072], P('dev', 'slab')
The draws below stay inside these ranges and needn't reach their ends.
All inputs are finite; a program needn't handle non-finite values.
Results may differ from the reference program's by a relative error of at most 0.0029.
Values may be sent and summed in bfloat16 or wider, within the bound.
No kernel may reach another device: no remote copies, remote signals or barrier semaphores. Data moves between devices by JAX's collectives and lax.ppermute only.
A program may use at most 128 MiB of HBM per device.

```python
import jax
import jax.numpy as jnp
from jax import lax

W = 3072
YB = 384
TAPS = 4
NDEF = 8
ZD = 4
TILTS = 32
SLABS = 4
Z = 16


def touch_ends(result, own_key, least, high):
    shape = result.shape
    place = [jax.random.randint(jax.random.fold_in(own_key, axis), (), 0, shape[axis]) for axis in range(len(shape))]
    result = result.at[tuple(place)].set(least)
    longest = shape.index(max(shape))
    place[longest] = (place[longest] + 1) % shape[longest]
    return result.at[tuple(place)].set(high)


def block_scale(stream_key, shape, shards, low, high):
    def one(position, blocks):
        draws = jax.random.uniform(jax.random.fold_in(jax.random.fold_in(stream_key, 6), position), (blocks,), jnp.float32, low / len(shards), high / len(shards))
        return jnp.repeat(jnp.exp(draws), shape[position] // blocks).reshape((-1,) + (1,) * (len(shape) - position - 1))

    gain = one(*shards[0])
    for cut in shards[1:]:
        gain = gain * one(*cut)
    return gain


def noise(own_key, extent, width, bound, pieces=(), kind=jnp.bfloat16):
    drawn = jax.random.normal(own_key, extent, jnp.float32) * width
    if len(pieces) > 0:
        drawn = block_scale(own_key, extent, pieces, -0.22, 0.18) * drawn
    return jnp.clip(drawn, min=-bound, max=bound).astype(kind)


def setup_inputs(seed: int = 0) -> dict:
    streams_of = jax.random.split(jax.random.key(seed), 7)
    tilts = noise(streams_of[0], (TILTS, YB, W), 1.0, 6.0, ((0, 32), (1, 4)))
    tilt_defocus = jnp.clip(1.0 + 2.0 * jax.random.uniform(streams_of[1], (TILTS,), jnp.float32) ** block_scale(streams_of[1], (TILTS,), ((0, 32),), -0.2, 0.2), 1.0, 3.0)
    defocus_table = jnp.clip(jax.random.uniform(streams_of[2], (NDEF,), jnp.float32, 0.2, 1.0), 0.2, 1.0)
    slab_pick = touch_ends(jax.random.randint(streams_of[3], (SLABS,), 0, NDEF), jax.random.fold_in(streams_of[3], 1), 0, NDEF - 1).astype(jnp.int32)
    interp_offset = touch_ends(jax.random.randint(streams_of[4], (TILTS, Z), 0 - W // 4, W // 4 + 1), jax.random.fold_in(streams_of[4], 1), 0 - W // 4, (W // 4 + 1) - 1).astype(jnp.int32)
    interp_weights = noise(streams_of[5], (TILTS, Z, TAPS), (TILTS * TAPS) ** -0.5, 0.5, ((1, 4),))
    return {"tilts": tilts, "tilt_defocus": tilt_defocus, "defocus_table": defocus_table, "slab_pick": slab_pick, "interp_offset": interp_offset, "interp_weights": interp_weights}


chi_scale = 200.0
phase_shift = 0.1


def signed_freq(count):
    counter = jnp.arange(count, dtype=jnp.int32)
    shifted = jnp.where(counter * 2 < count, counter, counter - count)
    return shifted.astype(jnp.float32) / count


def correct_tilt(pair):
    image, focus = pair
    freq_rows = signed_freq(YB)
    freq_cols = signed_freq(W)
    radius = freq_rows[:, None] ** 2 + freq_cols[None, :] ** 2
    response = -jnp.sin(chi_scale * focus * radius + phase_shift)
    spectrum = jnp.fft.fft2(image.astype(jnp.float32))
    restored = jnp.real(jnp.fft.ifft2(spectrum * response))
    return restored.astype(jnp.bfloat16)


def reference(tilts, tilt_defocus, defocus_table, slab_pick, interp_offset, interp_weights):
    margin = W // 4 + TAPS
    groups = []
    for group in range(SLABS):
        group_defocus = defocus_table[slab_pick[group]]
        focus_all = tilt_defocus + group_defocus
        filtered = lax.map(correct_tilt, (tilts, focus_all))
        padded = jnp.pad(filtered, ((0, 0), (0, 0), (margin, margin)))
        shifts = interp_offset[:, group * ZD:(group + 1) * ZD]
        weights = interp_weights[:, group * ZD:(group + 1) * ZD, :]

        def one_plane(pair):
            shift_col, weight_col = pair
            window = jax.vmap(lambda plane, start: lax.dynamic_slice_in_dim(plane, start, W + TAPS - 1, 1))(padded, (shift_col + margin).astype(jnp.int32))
            window = window.astype(jnp.float32)
            weight_col = weight_col.astype(jnp.float32)
            total = jnp.zeros((YB, W), jnp.float32)
            for tap_index in range(TAPS):
                total = total + jnp.einsum('tyx,t->yx', window[:, :, tap_index:tap_index + W], weight_col[:, tap_index])
            return total

        planes = lax.map(one_plane, (shifts.T, jnp.swapaxes(weights, 0, 1)))
        groups.append(jnp.swapaxes(planes, 0, 1))
    return jnp.concatenate(groups, axis=1)
```

```python
import math

import jax
import jax.numpy as jnp
import ml_dtypes
import numpy as np
from jax import lax
from jax.experimental import pallas as pl
from jax.experimental.pallas import tpu as pltpu
from jax.sharding import PartitionSpec as P

W = 3072
YB = 384
TAPS = 4
TILTS = 32
ZD = 4
XP = 24
XQ = 128
NJ = 12
ROWS = YB // TILTS
TILES = XP * ROWS // 16
LEFT = 6
BLOCKS = 38
GROUP = 4

chi_scale = 200.0
phase_shift = 0.1
root_half = math.sqrt(0.5)
sin_third = math.sqrt(0.75)


def split_np(table):
    high = table.astype(ml_dtypes.bfloat16)
    low = (table - high.astype(np.float64)).astype(ml_dtypes.bfloat16)
    return high, low


def x_tables():
    n2 = np.arange(XQ)
    k2 = np.arange(XQ)
    forward = np.zeros((NJ, 2 * XQ, 2 * XQ))
    inverse = np.zeros((NJ, 2 * XQ, 2 * XQ))
    for j in range(NJ):
        if j == 0:
            for half, k1 in enumerate((0, 12)):
                angle = 2 * np.pi * ((n2[:, None] * (k1 + XP * k2[None, :])) % W) / W
                cas = np.cos(angle) + np.sin(angle)
                cut = slice(half * XQ, (half + 1) * XQ)
                forward[j, cut, cut] = cas
                inverse[j, cut, cut] = cas.T / W
        else:
            angle = 2 * np.pi * ((n2[:, None] * (j + XP * k2[None, :])) % W) / W
            cos, sin = np.cos(angle), np.sin(angle)
            forward[j] = np.block([[cos, -sin], [sin, cos]])
            inverse[j] = np.block([[cos.T, sin.T], [-sin.T, cos.T]]) * (2.0 / W)
    return forward, inverse


def x_frequencies():
    k2 = np.arange(XQ)
    result = np.zeros((NJ, 2 * XQ))
    for j in range(NJ):
        first, second = (0, 12) if j == 0 else (j, j)
        for half, k1 in enumerate((first, second)):
            k = k1 + XP * k2
            result[j, half * XQ : (half + 1) * XQ] = np.where(2 * k < W, k, k - W) / W
    return result


def y_frequencies():
    a = np.arange(YB)
    return np.where(2 * a < YB, a, a - YB) / YB


def row_order():
    first = [ROWS * d + y for d in range(TILTS) for y in range(8)]
    second = [ROWS * d + y for d in range(TILTS) for y in range(8, ROWS)]
    return np.array(first + second)


def y_table():
    a = np.arange(YB)
    angle = 2 * np.pi * ((a[:, None] * a[None, :]) % YB) / YB
    return np.cos(angle) + np.sin(angle)


def real_eight(x):
    s0, d0 = x[0] + x[4], x[0] - x[4]
    s1, d1 = x[1] + x[5], x[1] - x[5]
    s2, d2 = x[2] + x[6], x[2] - x[6]
    s3, d3 = x[3] + x[7], x[3] - x[7]
    t0, t1 = s0 + s2, s1 + s3
    u = (d1 - d3) * root_half
    v = (d1 + d3) * root_half
    return {
        0: (t0 + t1, None),
        4: (t0 - t1, None),
        2: (s0 - s2, s3 - s1),
        1: (d0 + u, -(d2 + v)),
        3: (d0 - u, d2 - v),
    }


def forward_24(x):
    parts = [real_eight([x[(8 * a + 3 * b) % 24] for b in range(8)]) for a in range(3)]
    found = {}

    def put(ka, kb, value):
        for k in range(24):
            if k % 3 == ka % 3 and k % 8 == kb % 8:
                if k <= 12:
                    found[k] = value
                else:
                    re, im = value
                    found[24 - k] = (re, None if im is None else -im)

    for kb in (0, 4):
        p, q, r = (parts[a][kb][0] for a in range(3))
        total = q + r
        put(0, kb, (p + total, None))
        put(1, kb, (p - 0.5 * total, (r - q) * sin_third))
    for kb in (1, 2, 3):
        (pr, pi), (qr, qi), (rr, ri) = (parts[a][kb] for a in range(3))
        tr, ti = qr + rr, qi + ri
        put(0, kb, (pr + tr, pi + ti))
        mr, mi = pr - 0.5 * tr, pi - 0.5 * ti
        er, ei = (qr - rr) * sin_third, (qi - ri) * sin_third
        put(1, kb, (mr + ei, mi - er))
        put(2, kb, (mr - ei, mi + er))
    return found


def inverse_24(v):
    def get(ka, kb):
        k = next(i for i in range(24) if i % 3 == ka and i % 8 == kb)
        if k <= 12:
            return v[k]
        re, im = v[24 - k]
        return (re, -im)

    eights = [dict() for _ in range(3)]
    for kb in (0, 4):
        p = get(0, kb)[0]
        sr, si = get(1, kb)
        m = p - 0.5 * sr
        e = si * sin_third
        eights[0][kb] = (p + sr, None)
        eights[1][kb] = (m - e, None)
        eights[2][kb] = (m + e, None)
    for kb in (1, 2, 3):
        (pr, pi), (qr, qi), (rr, ri) = get(0, kb), get(1, kb), get(2, kb)
        tr, ti = qr + rr, qi + ri
        mr, mi = pr - 0.5 * tr, pi - 0.5 * ti
        er, ei = (qr - rr) * sin_third, (qi - ri) * sin_third
        eights[0][kb] = (pr + tr, pi + ti)
        eights[1][kb] = (mr - ei, mi + er)
        eights[2][kb] = (mr + ei, mi - er)
    out = [None] * 24
    for a in range(3):
        g = eights[a]
        g0, g4 = g[0][0], g[4][0]
        (r1, i1), (r2, i2), (r3, i3) = g[1], g[2], g[3]
        c0, c1 = g0 + g4, g0 - g4
        e0, e2 = c0 + r2, c0 - r2
        o0, o2 = r1 + r3, i1 - i3
        e1, e3 = c1 - i2, c1 + i2
        da, db = (r1 - r3) * root_half, (i1 + i3) * root_half
        o1, o3 = da - db, -(da + db)
        values = [e0 + o0, e1 + o1, e2 - o2, e3 + o3, e0 - o0, e1 - o1, e2 + o2, e3 - o3]
        for b in range(8):
            out[(8 * a + 3 * b) % 24] = values[b]
    return out


def split(value):
    high = value.astype(jnp.bfloat16)
    low = (value - high.astype(jnp.float32)).astype(jnp.bfloat16)
    return high, low


def dot(a, b):
    return jnp.dot(a, b, preferred_element_type=jnp.float32)


STRIP = 16
CHUNK = 128


def filter_kernel(x_ref, fh_ref, fl_ref, ih_ref, il_ref, ah_ref, al_ref, gx_ref, out_ref,
                  vh, vl, uh, ul, back):
    j = pl.program_id(0)

    @pl.when(j == 0)
    def _():
        def strip(i, carry):
            rows = pl.ds(pl.multiple_of(i * STRIP, STRIP), STRIP)
            blocks = [
                x_ref[rows, b * XQ : (b + 1) * XQ].astype(jnp.float32) for b in range(XP)
            ]
            found = forward_24(blocks)
            for jj in range(NJ):
                if jj == 0:
                    pair = (found[0][0], found[12][0])
                else:
                    pair = found[jj]
                for half in range(2):
                    high, low = split(pair[half])
                    vh[jj, rows, half * XQ : (half + 1) * XQ] = high
                    vl[jj, rows, half * XQ : (half + 1) * XQ] = low
            return carry

        lax.fori_loop(0, YB // STRIP, strip, 0)

    for c in range(YB // CHUNK):
        rows = slice(c * CHUNK, (c + 1) * CHUNK)
        high, low = vh[j, rows, :], vl[j, rows, :]
        u = dot(high, fh_ref[0]) + dot(low, fh_ref[0]) + dot(high, fl_ref[0])
        uh[rows, :], ul[rows, :] = split(u)
    gain = gx_ref[0]
    for c in range(YB // CHUNK):
        rows = slice(c * CHUNK, (c + 1) * CHUNK)
        total = None
        for r in range(2):
            cut = slice(r * YB + c * CHUNK, r * YB + (c + 1) * CHUNK)
            y = dot(ah_ref[cut, :], uh[...]) + dot(al_ref[cut, :], uh[...])
            y = y + dot(ah_ref[cut, :], ul[...])
            y = y * gain[r : r + 1, :]
            total = y if total is None else total + y
        high, low = split(total)
        z = dot(high, ih_ref[0]) + dot(low, ih_ref[0]) + dot(high, il_ref[0])
        back[j, rows, :] = z

    def blocks_of(start):
        rows = pl.ds(pl.multiple_of(start, 8), 8)
        v = {}
        for jj in range(NJ):
            first, second = back[jj, rows, 0:XQ], back[jj, rows, XQ : 2 * XQ]
            if jj == 0:
                v[0], v[12] = (first, None), (second, None)
            else:
                v[jj] = (first, second)
        return inverse_24(v)

    @pl.when(j == NJ - 1)
    def _():
        def first_part(d, carry):
            values = blocks_of(d * 8)
            for pair in range(XP // 2):
                tile = jnp.concatenate([values[2 * pair], values[2 * pair + 1]], axis=0)
                out_ref[d, pair] = tile.astype(jnp.bfloat16)
            return carry

        lax.fori_loop(0, TILTS, first_part, 0)

        def second_part(i, carry):
            values = blocks_of(8 * TILTS + i * 8)
            for half in range(2):
                for quad in range(XP // 4):
                    tile = jnp.concatenate(
                        [values[4 * quad + n][4 * half : 4 * half + 4] for n in range(4)], axis=0
                    )
                    out_ref[2 * i + half, XP // 2 + quad] = tile.astype(jnp.bfloat16)
            return carry

        lax.fori_loop(0, TILTS // 2, second_part, 0)


def run_filter(whole, tables, ah, al, gx):
    fh, fl, ih, il = tables
    table_spec = pl.BlockSpec((1, 2 * XQ, 2 * XQ), lambda j: (j, 0, 0))
    return pl.pallas_call(
        filter_kernel,
        grid=(NJ,),
        in_specs=[
            pl.BlockSpec((YB, W), lambda j: (0, 0)),
            table_spec,
            table_spec,
            table_spec,
            table_spec,
            pl.BlockSpec((2 * YB, YB), lambda j: (0, 0)),
            pl.BlockSpec((2 * YB, YB), lambda j: (0, 0)),
            pl.BlockSpec((1, 2, 2 * XQ), lambda j: (j, 0, 0)),
        ],
        out_specs=pl.BlockSpec((TILTS, TILES, 16, XQ), lambda j: (0, 0, 0, 0)),
        out_shape=jax.ShapeDtypeStruct((TILTS, TILES, 16, XQ), jnp.bfloat16),
        scratch_shapes=[
            pltpu.VMEM((NJ, YB, 2 * XQ), jnp.bfloat16),
            pltpu.VMEM((NJ, YB, 2 * XQ), jnp.bfloat16),
            pltpu.VMEM((YB, 2 * XQ), jnp.bfloat16),
            pltpu.VMEM((YB, 2 * XQ), jnp.bfloat16),
            pltpu.VMEM((NJ, YB, 2 * XQ), jnp.float32),
        ],
        compiler_params=pltpu.CompilerParams(
            dimension_semantics=("arbitrary",), vmem_limit_bytes=56 * 2**20
        ),
    )(whole, fh, fl, ih, il, ah, al, gx)


def band_kernel(off_ref, weight_ref, out_ref):
    step = pl.program_id(0)
    distance = lax.broadcasted_iota(jnp.int32, (2 * XQ, XQ), 0) - lax.broadcasted_iota(
        jnp.int32, (2 * XQ, XQ), 1
    )
    for z in range(ZD):
        for g in range(GROUP):
            t = step * GROUP + g
            shift = off_ref[t, z] & (XQ - 1)
            moved = distance - shift
            band = jnp.zeros((2 * XQ, XQ), jnp.float32)
            for tap in range(TAPS):
                band = jnp.where(moved == tap, weight_ref[t, z * TAPS + tap], band)
            out_ref[0, z, g] = band.astype(jnp.bfloat16)


def run_band(off, weights):
    steps = TILTS // GROUP
    return pl.pallas_call(
        band_kernel,
        grid=(steps,),
        in_specs=[
            pl.BlockSpec(memory_space=pltpu.SMEM),
            pl.BlockSpec(memory_space=pltpu.SMEM),
        ],
        out_specs=pl.BlockSpec((1, ZD, GROUP, 2 * XQ, XQ), lambda i: (i, 0, 0, 0, 0)),
        out_shape=jax.ShapeDtypeStruct((steps, ZD, GROUP, 2 * XQ, XQ), jnp.bfloat16),
        compiler_params=pltpu.CompilerParams(dimension_semantics=("arbitrary",)),
    )(off, weights)


def project_kernel(off_ref, weight_ref, x_ref, band_ref, out_ref, padded, total):
    step = pl.program_id(0)

    @pl.when(step == 0)
    def _():
        padded[...] = jnp.zeros_like(padded)
        total[...] = jnp.zeros_like(total)

    for g in range(GROUP):
        for quad in range(XP // 4):
            tail = x_ref[g, XP // 2 + quad].astype(jnp.float32)
            for half in range(2):
                head = x_ref[g, 2 * quad + half].astype(jnp.float32)
                for n in range(2):
                    block = 4 * quad + 2 * half + n
                    part = tail[4 * (2 * half + n) : 4 * (2 * half + n) + 4]
                    tile = jnp.concatenate(
                        [head[8 * n : 8 * n + 8], part, jnp.zeros((4, XQ), jnp.float32)], axis=0
                    )
                    padded[g, LEFT + block] = tile.astype(jnp.bfloat16)

    def window(g, start):
        return padded[g, pl.ds(start, XP)].reshape(XP * 16, XQ)

    for z in range(ZD):
        parts = []
        for g in range(GROUP):
            start = (off_ref[step * GROUP + g, z] >> 7) + LEFT
            parts.append(window(g, start))
            parts.append(window(g, start + 1))
        left = jnp.concatenate(parts, axis=1)
        band = band_ref[0, z].reshape(GROUP * 2 * XQ, XQ)
        total[z] += dot(left, band)

    for g in range(GROUP):
        t = step * GROUP + g
        for z in range(ZD):
            shift = off_ref[t, z] & (XQ - 1)

            @pl.when(shift > XQ - TAPS + 1)
            def _():
                moved = (
                    lax.broadcasted_iota(jnp.int32, (XQ, XQ), 0)
                    - lax.broadcasted_iota(jnp.int32, (XQ, XQ), 1)
                    + (2 * XQ - shift)
                )
                band = jnp.zeros((XQ, XQ), jnp.float32)
                for tap in range(TAPS):
                    band = jnp.where(moved == tap, weight_ref[t, z * TAPS + tap], band)
                start = (off_ref[t, z] >> 7) + LEFT
                total[z] += dot(window(g, start + 2), band.astype(jnp.bfloat16))

    @pl.when(step == pl.num_programs(0) - 1)
    def _():
        for z in range(ZD):
            for b in range(XP):
                out_ref[:, z, b * XQ : (b + 1) * XQ] = total[z, b * 16 : b * 16 + ROWS, :]


def run_project(off, weights, moved, bands):
    steps = TILTS // GROUP
    return pl.pallas_call(
        project_kernel,
        grid=(steps,),
        in_specs=[
            pl.BlockSpec(memory_space=pltpu.SMEM),
            pl.BlockSpec(memory_space=pltpu.SMEM),
            pl.BlockSpec((GROUP, TILES, 16, XQ), lambda i: (i, 0, 0, 0)),
            pl.BlockSpec((1, ZD, GROUP, 2 * XQ, XQ), lambda i: (i, 0, 0, 0, 0)),
        ],
        out_specs=pl.BlockSpec((ROWS, ZD, W), lambda i: (0, 0, 0)),
        out_shape=jax.ShapeDtypeStruct((ROWS, ZD, W), jnp.float32),
        scratch_shapes=[
            pltpu.VMEM((GROUP, BLOCKS, 16, XQ), jnp.bfloat16),
            pltpu.VMEM((ZD, XP * 16, XQ), jnp.float32),
        ],
        compiler_params=pltpu.CompilerParams(
            dimension_semantics=("arbitrary",), vmem_limit_bytes=48 * 2**20
        ),
    )(off, weights, moved, bands)


def responses(focus):
    scale = chi_scale * focus
    fy = jnp.asarray(y_frequencies(), jnp.float32)
    angle_y = scale * (fy * fy) + phase_shift
    fx = jnp.asarray(x_frequencies(), jnp.float32)
    angle_x = scale * (fx * fx)
    table = y_table()
    left = jnp.asarray(table[row_order()] / YB, jnp.float32)
    right = jnp.asarray(table, jnp.float32)
    side = jnp.concatenate([left * -jnp.sin(angle_y), left * -jnp.cos(angle_y)], axis=0)
    mixed = jnp.dot(side, right, precision=lax.Precision.HIGHEST)
    rounded = lax.reduce_precision(mixed, exponent_bits=8, mantissa_bits=7)
    ah, al = rounded.astype(jnp.bfloat16), (mixed - rounded).astype(jnp.bfloat16)
    gx = jnp.stack([jnp.cos(angle_x), jnp.sin(angle_x)], axis=1)
    return ah, al, gx


def body(tilts, tilt_defocus, defocus_table, slab_pick, interp_offset, interp_weights):
    entries = jnp.arange(defocus_table.shape[0], dtype=jnp.int32)
    group_defocus = jnp.sum(jnp.where(entries == slab_pick[0], defocus_table, 0.0))
    focus = tilt_defocus[0] + group_defocus
    whole = lax.all_gather(tilts, "slab", axis=1, tiled=True)
    ah, al, gx = responses(focus)
    weights = interp_weights.astype(jnp.float32).reshape(TILTS, ZD * TAPS)
    bands = run_band(interp_offset, weights)
    forward, inverse = x_tables()
    tables = [jnp.asarray(t) for pair in (split_np(forward), split_np(inverse)) for t in pair]
    filtered = run_filter(whole[0], tables, ah, al, gx)
    moved = lax.all_to_all(filtered, "dev", split_axis=0, concat_axis=0, tiled=True)
    return run_project(interp_offset, weights, moved, bands)


def solution(mesh):
    in_specs = (
        P("dev", "slab", None),
        P("dev"),
        P(),
        P("slab"),
        P(None, "slab"),
        P(None, "slab", None),
    )
    out_specs = P("dev", "slab", None)
    return jax.shard_map(body, mesh=mesh, in_specs=in_specs, out_specs=out_specs, check_vma=False)
```

```python
import math

import jax
import jax.numpy as jnp
import ml_dtypes
import numpy as np
from jax import lax
from jax.experimental import pallas as pl
from jax.experimental.pallas import tpu as pltpu
from jax.sharding import PartitionSpec as P

W = 3072
YB = 384
TAPS = 4
TILTS = 32
ZD = 4
XP = 24
XQ = 128
NJ = 12
ROWS = YB // TILTS
PARTS = ((0, 8), (8, 4))
TILES = XP * ROWS // 16
HALF = YB // 2
QUARTER = YB // 4
DEPTH = 256
LEFT = 8
SPAN = 40
GROUP = 4

chi_scale = 200.0
phase_shift = 0.1
root_half = math.sqrt(0.5)
sin_third = math.sqrt(0.75)


def split_np(table):
    high = table.astype(ml_dtypes.bfloat16)
    low = (table - high.astype(np.float64)).astype(ml_dtypes.bfloat16)
    return high, low


def x_tables():
    n2 = np.arange(XQ)
    k2 = np.arange(XQ)
    forward = np.zeros((NJ, 2 * XQ, 2 * XQ))
    inverse = np.zeros((NJ, 2 * XQ, 2 * XQ))
    for j in range(NJ):
        if j == 0:
            for half, k1 in enumerate((0, 12)):
                angle = 2 * np.pi * ((n2[:, None] * (k1 + XP * k2[None, :])) % W) / W
                cas = np.cos(angle) + np.sin(angle)
                cut = slice(half * XQ, (half + 1) * XQ)
                forward[j, cut, cut] = cas
                inverse[j, cut, cut] = cas.T / W
        else:
            angle = 2 * np.pi * ((n2[:, None] * (j + XP * k2[None, :])) % W) / W
            cos, sin = np.cos(angle), np.sin(angle)
            forward[j] = np.block([[cos, -sin], [sin, cos]])
            inverse[j] = np.block([[cos.T, sin.T], [-sin.T, cos.T]]) * (2.0 / W)
    return forward, inverse


def x_frequencies():
    k2 = np.arange(XQ)
    result = np.zeros((NJ, 2 * XQ))
    for j in range(NJ):
        first, second = (0, 12) if j == 0 else (j, j)
        for half, k1 in enumerate((first, second)):
            k = k1 + XP * k2
            result[j, half * XQ : (half + 1) * XQ] = np.where(2 * k < W, k, k - W) / W
    return result


def y_frequencies():
    a = np.arange(YB)
    return np.where(2 * a < YB, a, a - YB) / YB


def y_tables():
    y = np.arange(HALF)
    wanted = np.array(
        [
            ROWS * d + first + i
            for first, count in PARTS
            for d in range(TILTS // 2)
            for i in range(count)
        ]
    )
    left, right = [], []
    for odd in range(2):
        a = np.arange(odd, YB, 2)

        def cas(rows):
            angle = 2 * np.pi * ((rows[:, None] * a[None, :]) % YB) / YB
            return np.cos(angle) + np.sin(angle)

        left.append(cas(wanted) / YB)
        given = cas(y).T
        swapped = np.concatenate([given[:, QUARTER:], given[:, :QUARTER]], axis=1)
        right.append([given, swapped])
    return np.array(left, np.float32), np.array(right, np.float32)


def real_eight(x):
    s0, d0 = x[0] + x[4], x[0] - x[4]
    s1, d1 = x[1] + x[5], x[1] - x[5]
    s2, d2 = x[2] + x[6], x[2] - x[6]
    s3, d3 = x[3] + x[7], x[3] - x[7]
    t0, t1 = s0 + s2, s1 + s3
    u = (d1 - d3) * root_half
    v = (d1 + d3) * root_half
    return {
        0: (t0 + t1, None),
        4: (t0 - t1, None),
        2: (s0 - s2, s3 - s1),
        1: (d0 + u, -(d2 + v)),
        3: (d0 - u, d2 - v),
    }


def forward_24(x):
    parts = [real_eight([x[(8 * a + 3 * b) % 24] for b in range(8)]) for a in range(3)]
    found = {}

    def put(ka, kb, value):
        for k in range(24):
            if k % 3 == ka % 3 and k % 8 == kb % 8:
                if k <= 12:
                    found[k] = value
                else:
                    re, im = value
                    found[24 - k] = (re, None if im is None else -im)

    for kb in (0, 4):
        p, q, r = (parts[a][kb][0] for a in range(3))
        total = q + r
        put(0, kb, (p + total, None))
        put(1, kb, (p - 0.5 * total, (r - q) * sin_third))
    for kb in (1, 2, 3):
        (pr, pi), (qr, qi), (rr, ri) = (parts[a][kb] for a in range(3))
        tr, ti = qr + rr, qi + ri
        put(0, kb, (pr + tr, pi + ti))
        mr, mi = pr - 0.5 * tr, pi - 0.5 * ti
        er, ei = (qr - rr) * sin_third, (qi - ri) * sin_third
        put(1, kb, (mr + ei, mi - er))
        put(2, kb, (mr - ei, mi + er))
    return found


def inverse_24(v):
    def get(ka, kb):
        k = next(i for i in range(24) if i % 3 == ka and i % 8 == kb)
        if k <= 12:
            return v[k]
        re, im = v[24 - k]
        return (re, -im)

    eights = [dict() for _ in range(3)]
    for kb in (0, 4):
        p = get(0, kb)[0]
        sr, si = get(1, kb)
        m = p - 0.5 * sr
        e = si * sin_third
        eights[0][kb] = (p + sr, None)
        eights[1][kb] = (m - e, None)
        eights[2][kb] = (m + e, None)
    for kb in (1, 2, 3):
        (pr, pi), (qr, qi), (rr, ri) = get(0, kb), get(1, kb), get(2, kb)
        tr, ti = qr + rr, qi + ri
        mr, mi = pr - 0.5 * tr, pi - 0.5 * ti
        er, ei = (qr - rr) * sin_third, (qi - ri) * sin_third
        eights[0][kb] = (pr + tr, pi + ti)
        eights[1][kb] = (mr - ei, mi + er)
        eights[2][kb] = (mr + ei, mi - er)
    out = [None] * 24
    for a in range(3):
        g = eights[a]
        g0, g4 = g[0][0], g[4][0]
        (r1, i1), (r2, i2), (r3, i3) = g[1], g[2], g[3]
        c0, c1 = g0 + g4, g0 - g4
        e0, e2 = c0 + r2, c0 - r2
        o0, o2 = r1 + r3, i1 - i3
        e1, e3 = c1 - i2, c1 + i2
        da, db = (r1 - r3) * root_half, (i1 + i3) * root_half
        o1, o3 = da - db, -(da + db)
        values = [e0 + o0, e1 + o1, e2 - o2, e3 + o3, e0 - o0, e1 - o1, e2 + o2, e3 - o3]
        for b in range(8):
            out[(8 * a + 3 * b) % 24] = values[b]
    return out


def split(value):
    high = value.astype(jnp.bfloat16)
    low = (value - high.astype(jnp.float32)).astype(jnp.bfloat16)
    return high, low


def three_products(high, low, table_high, table_low):
    left = jnp.concatenate([high, low, high], axis=1)
    right = jnp.concatenate([table_high, table_high, table_low], axis=0)
    return jnp.dot(left, right, preferred_element_type=jnp.float32)


STRIP = 16


def load_strips(x_refs, vh, vl):
    for n, x_ref in enumerate(x_refs):

        def strip(i, carry):
            rows = pl.ds(pl.multiple_of(i * STRIP, STRIP), STRIP)
            target = pl.ds(pl.multiple_of(n * QUARTER + i * STRIP, STRIP), STRIP)
            blocks = [
                x_ref[rows, b * XQ : (b + 1) * XQ].astype(jnp.float32) for b in range(XP)
            ]
            found = forward_24(blocks)
            for jj in range(NJ):
                if jj == 0:
                    pair = (found[0][0], found[12][0])
                else:
                    pair = found[jj]
                for half in range(2):
                    high, low = split(pair[half])
                    vh[jj, target, half * XQ : (half + 1) * XQ] = high
                    vl[jj, target, half * XQ : (half + 1) * XQ] = low
            return carry

        lax.fori_loop(0, QUARTER // STRIP, strip, 0)


def near_kernel(focus_ref, slab_ref, xa_ref, xb_ref, fh_ref, fl_ref, left_ref, right_ref, fy_ref,
                fx_ref, out_ref, mix_ref, gain_ref, vh, vl):
    load_strips((xa_ref, xb_ref), vh, vl)

    def column(j, carry):
        out_ref[j] = three_products(vh[j], vl[j], fh_ref[j], fl_ref[j])
        return carry

    lax.fori_loop(0, NJ, column, 0)
    scale = chi_scale * focus_ref[0]
    slab = slab_ref[0]
    angle_x = scale * (fx_ref[...] * fx_ref[...])
    cos_x, sin_x = jnp.cos(angle_x), jnp.sin(angle_x)
    for j in range(NJ):
        gain_ref[j] = jnp.concatenate([cos_x[j : j + 1], sin_x[j : j + 1]], axis=0)
    for odd in range(2):
        fy = fy_ref[odd : odd + 1, :]
        angle_y = scale * (fy * fy) + phase_shift
        left = left_ref[odd]
        side = jnp.concatenate([left * -jnp.sin(angle_y), left * -jnp.cos(angle_y)], axis=0)
        right = right_ref[odd, slab & 1]
        mixed = jnp.dot(
            side, right, precision=lax.Precision.HIGHEST, preferred_element_type=jnp.float32
        )
        if odd:
            mixed = mixed * jnp.where(slab < 2, 1.0, -1.0)
        empty = jnp.zeros((YB, DEPTH - HALF), jnp.float32)
        high, low = split(jnp.concatenate([mixed, empty], axis=1))
        mix_ref[odd] = jnp.concatenate([high, low, high], axis=1)


def parameters():
    return pltpu.CompilerParams(vmem_limit_bytes=63 * 2**20)


def scalar_spec():
    return pl.BlockSpec(memory_space=pltpu.SMEM)


def halves():
    return [pltpu.VMEM((NJ, HALF, 2 * XQ), jnp.bfloat16)] * 2


def run_near(focus, slab, xa, xb, fh, fl):
    left, right = y_tables()
    fy = y_frequencies()
    fy = np.stack([fy[0::2], fy[1::2]]).astype(np.float32)
    fx = x_frequencies().astype(np.float32)
    return pl.pallas_call(
        near_kernel,
        in_specs=[scalar_spec()] * 2 + [pl.BlockSpec(memory_space=pltpu.VMEM)] * 8,
        out_shape=[
            jax.ShapeDtypeStruct((NJ, HALF, 2 * XQ), jnp.float32),
            jax.ShapeDtypeStruct((2, YB, 3 * DEPTH), jnp.bfloat16),
            jax.ShapeDtypeStruct((NJ, 2, 2 * XQ), jnp.float32),
        ],
        scratch_shapes=halves(),
        compiler_params=parameters(),
        name="near",
    )(focus, slab, xa, xb, fh, fl, *(jnp.asarray(t) for t in (left, right, fy, fx)))


def main_kernel(xa_any, xb_any, near_any, fh_any, fl_any, mix_any, gain_any, ih_any, il_any,
                out_any, xa, xb, near, fh, fl, mix, gain, ih, il, vh, vl, back, out,
                early, late, sent):
    first = [(xa_any, xa), (xb_any, xb), (mix_any, mix), (gain_any, gain)]
    copies = [pltpu.make_async_copy(a, b, early.at[i]) for i, (a, b) in enumerate(first)]
    for copy in copies[:2]:
        copy.start()
    streams = [(near_any, near), (fh_any, fh), (fl_any, fl), (ih_any, ih), (il_any, il)]

    def stream(n, j):
        source, target = streams[n]
        return pltpu.make_async_copy(source.at[j], target.at[j], late.at[n, j])

    for j in range(NJ):
        for n in range(len(streams)):
            stream(n, j).start()
        if j == 0:
            for copy in copies[2:]:
                copy.start()
    for copy in copies[:2]:
        copy.wait()
    load_strips((xa, xb), vh, vl)
    for copy in copies[2:]:
        copy.wait()
    empty = jnp.zeros((DEPTH - HALF, 2 * XQ), jnp.bfloat16)

    def column(j, carry):
        for n in range(len(streams)):
            stream(n, j).wait()
        far = three_products(vh[j], vl[j], fh[j], fl[j])
        here = near[j]
        factors = gain[j]

        def mixed(odd, value):
            high, low = split(value)
            right = jnp.concatenate([high, empty, high, empty, low, empty], axis=0)
            y = jnp.dot(mix[odd], right, preferred_element_type=jnp.float32)
            return y[:HALF] * factors[0:1] + y[HALF:] * factors[1:2]

        even = mixed(0, here + far)
        odd = mixed(1, here - far)
        high, low = split(jnp.concatenate([even + odd, even - odd], axis=0))
        back[j] = three_products(high, low, ih[j], il[j])
        return carry

    lax.fori_loop(0, NJ, column, 0)

    def blocks_of(start):
        cut = pl.ds(pl.multiple_of(start, 8), 8)
        v = {}
        for jj in range(NJ):
            one, two = back[jj, cut, 0:XQ], back[jj, cut, XQ : 2 * XQ]
            if jj == 0:
                v[0], v[12] = (one, None), (two, None)
            else:
                v[jj] = (one, two)
        return inverse_24(v)

    devices = TILTS // 2
    for half in range(2):
        low_row, low_tile = half * HALF, 0
        for _, count in PARTS:
            per_strip, per_tile = 8 // count, 16 // count

            def strip(i, carry):
                values = blocks_of(low_row + i * 8)
                for part in range(per_strip):
                    cut = slice(part * count, (part + 1) * count)
                    for tile in range(XP // per_tile):
                        pieces = [values[per_tile * tile + n][cut] for n in range(per_tile)]
                        joined = jnp.concatenate(pieces, axis=0)
                        place = half * devices + i * per_strip + part
                        out[place, low_tile + tile] = joined.astype(jnp.bfloat16)
                return carry

            lax.fori_loop(0, devices // per_strip, strip, 0)
            low_row += devices * count
            low_tile += XP // per_tile
        cut = pl.ds(half * devices, devices)
        pltpu.make_async_copy(out.at[cut], out_any.at[cut], sent.at[half]).start()
    for half in range(2):
        cut = pl.ds(half * devices, devices)
        pltpu.make_async_copy(out.at[cut], out_any.at[cut], sent.at[half]).wait()


def run_main(xa, xb, near, mix, gain, fh, fl, ih, il):
    shape = (TILTS, TILES, 16, XQ)
    args = (xa, xb, near, fh, fl, mix, gain, ih, il)
    return pl.pallas_call(
        main_kernel,
        in_specs=[pl.BlockSpec(memory_space=pl.ANY)] * len(args),
        out_specs=pl.BlockSpec(memory_space=pl.ANY),
        out_shape=jax.ShapeDtypeStruct(shape, jnp.bfloat16),
        scratch_shapes=[pltpu.VMEM(a.shape, a.dtype) for a in args]
        + halves()
        + [
            pltpu.VMEM((NJ, YB, 2 * XQ), jnp.float32),
            pltpu.VMEM(shape, jnp.bfloat16),
            pltpu.SemaphoreType.DMA((4,)),
            pltpu.SemaphoreType.DMA((5, NJ)),
            pltpu.SemaphoreType.DMA((2,)),
        ],
        compiler_params=parameters(),
        name="main",
    )(*args)


def band_kernel(off_ref, weight_ref, out_ref):
    step = pl.program_id(0)
    distance = lax.broadcasted_iota(jnp.int32, (2 * XQ, XQ), 0) - lax.broadcasted_iota(
        jnp.int32, (2 * XQ, XQ), 1
    )
    for z in range(ZD):
        for g in range(GROUP):
            t = step * GROUP + g
            shift = off_ref[t, z] & (XQ - 1)
            moved = distance - shift
            band = jnp.zeros((2 * XQ, XQ), jnp.float32)
            for tap in range(TAPS):
                band = jnp.where(moved == tap, weight_ref[t, z * TAPS + tap], band)
            out_ref[0, z, g] = band.astype(jnp.bfloat16)


def run_band(off, weights):
    steps = TILTS // GROUP
    return pl.pallas_call(
        band_kernel,
        grid=(steps,),
        in_specs=[
            pl.BlockSpec(memory_space=pltpu.SMEM),
            pl.BlockSpec(memory_space=pltpu.SMEM),
        ],
        out_specs=pl.BlockSpec((1, ZD, GROUP, 2 * XQ, XQ), lambda i: (i, 0, 0, 0, 0)),
        out_shape=jax.ShapeDtypeStruct((steps, ZD, GROUP, 2 * XQ, XQ), jnp.bfloat16),
        compiler_params=pltpu.CompilerParams(dimension_semantics=("arbitrary",)),
    )(off, weights)


def project_kernel(off_ref, weight_ref, x_any, band_any, out_ref, x, bands, arrived, wide, narrow,
                   total):
    steps = TILTS // GROUP

    def fetch(i):
        some = pl.ds(i * GROUP, GROUP)
        return (
            pltpu.make_async_copy(x_any.at[some], x.at[some], arrived.at[0, i]),
            pltpu.make_async_copy(band_any.at[i], bands.at[i], arrived.at[1, i]),
        )

    for i in range(steps):
        for copy in fetch(i):
            copy.start()
    wide[...] = jnp.zeros_like(wide)
    narrow[...] = jnp.zeros_like(narrow)
    total[...] = jnp.zeros_like(total)
    layouts = []
    base = 0
    for padded, (_, count) in zip((wide, narrow), PARTS):
        per_tile = 16 // count
        layouts.append((padded, count, per_tile, XP // per_tile, base))
        base += XP // per_tile

    def window(g, start):
        pieces = []
        for padded, count, per_tile, tiles, _ in layouts:
            log_tile = per_tile.bit_length() - 1
            piece = padded[start & (per_tile - 1), g, pl.ds(start >> log_tile, tiles)]
            pieces.append(piece.reshape(tiles * 16, XQ))
        return jnp.concatenate(pieces, axis=0)

    def step(i, carry):
        for copy in fetch(i):
            copy.wait()
        for g in range(GROUP):
            t = i * GROUP + g
            for padded, count, per_tile, tiles, base in layouts:
                lead = LEFT // per_tile
                rows = [x[t, base + p].astype(jnp.float32) for p in range(tiles)]
                empty = jnp.zeros((16, XQ), jnp.float32)
                for p in range(tiles):
                    padded[0, g, lead + p] = x[t, base + p]
                for m in range(1, per_tile):
                    for p in range(-1, tiles):
                        here = rows[p] if p >= 0 else empty
                        later = rows[p + 1] if p + 1 < tiles else empty
                        tile = jnp.concatenate([here[m * count :], later[: m * count]], axis=0)
                        padded[m, g, lead + p] = tile.astype(jnp.bfloat16)
        for z in range(ZD):
            parts = []
            for g in range(GROUP):
                start = (off_ref[i * GROUP + g, z] >> 7) + LEFT
                parts.append(window(g, start))
                parts.append(window(g, start + 1))
            left = jnp.concatenate(parts, axis=1)
            band = bands[i, z].reshape(GROUP * 2 * XQ, XQ)
            total[z] += jnp.dot(left, band, preferred_element_type=jnp.float32)

        for g in range(GROUP):
            t = i * GROUP + g
            for z in range(ZD):
                shift = off_ref[t, z] & (XQ - 1)

                @pl.when(shift > XQ - TAPS + 1)
                def _():
                    moved = (
                        lax.broadcasted_iota(jnp.int32, (XQ, XQ), 0)
                        - lax.broadcasted_iota(jnp.int32, (XQ, XQ), 1)
                        + (2 * XQ - shift)
                    )
                    band = jnp.zeros((XQ, XQ), jnp.float32)
                    for tap in range(TAPS):
                        band = jnp.where(moved == tap, weight_ref[t, z * TAPS + tap], band)
                    start = (off_ref[t, z] >> 7) + LEFT
                    total[z] += jnp.dot(
                        window(g, start + 2),
                        band.astype(jnp.bfloat16),
                        preferred_element_type=jnp.float32,
                    )

        return carry

    lax.fori_loop(0, steps, step, 0)
    for z in range(ZD):
        for (first, count), (_, _, _, _, base) in zip(PARTS, layouts):
            for b in range(XP):
                row = base * 16 + b * count
                out_ref[first : first + count, z, b * XQ : (b + 1) * XQ] = total[
                    z, row : row + count, :
                ]


def run_project(off, weights, moved, bands):
    steps = TILTS // GROUP
    return pl.pallas_call(
        project_kernel,
        in_specs=[scalar_spec()] * 2 + [pl.BlockSpec(memory_space=pl.ANY)] * 2,
        out_shape=jax.ShapeDtypeStruct((ROWS, ZD, W), jnp.float32),
        scratch_shapes=[
            pltpu.VMEM(moved.shape, moved.dtype),
            pltpu.VMEM(bands.shape, bands.dtype),
            pltpu.SemaphoreType.DMA((2, steps)),
            pltpu.VMEM((2, GROUP, SPAN // 2, 16, XQ), jnp.bfloat16),
            pltpu.VMEM((4, GROUP, SPAN // 4, 16, XQ), jnp.bfloat16),
            pltpu.VMEM((ZD, TILES * 16, XQ), jnp.float32),
        ],
        compiler_params=parameters(),
        name="project",
    )(off, weights, moved, bands)


def body(tilts, tilt_defocus, defocus_table, slab_pick, interp_offset, interp_weights):
    def swap(block, bit):
        return lax.ppermute(block, "slab", [(i, i ^ bit) for i in range(4)])

    own = tilts[0]
    beside = swap(own, 1)
    across = swap(own, 2)
    entries = jnp.arange(defocus_table.shape[0], dtype=jnp.int32)
    group_defocus = jnp.sum(jnp.where(entries == slab_pick[0], defocus_table, 0.0))
    focus = tilt_defocus + group_defocus
    slab = lax.axis_index("slab").astype(jnp.int32).reshape(1)
    forward, inverse = x_tables()
    fh, fl = (jnp.asarray(t) for t in split_np(forward))
    ih, il = (jnp.asarray(t) for t in split_np(inverse))
    near, mix, gain = run_near(focus, slab, own, beside, fh, fl)
    near, across = lax.optimization_barrier((near, across))
    opposite = swap(across, 1)
    weights = interp_weights.astype(jnp.float32).reshape(TILTS, ZD * TAPS)
    bands = run_band(interp_offset, weights)
    filtered = run_main(across, opposite, near, mix, gain, fh, fl, ih, il)
    moved = lax.all_to_all(filtered, "dev", split_axis=0, concat_axis=0, tiled=True)
    return run_project(interp_offset, weights, moved, bands)


def solution(mesh):
    in_specs = (
        P("dev", "slab", None),
        P("dev"),
        P(),
        P("slab"),
        P(None, "slab"),
        P(None, "slab", None),
    )
    out_specs = P("dev", "slab", None)
    return jax.shard_map(body, mesh=mesh, in_specs=in_specs, out_specs=out_specs, check_vma=False)
```

```python
import math

import jax
import jax.numpy as jnp
import ml_dtypes
import numpy as np
from jax import lax
from jax.experimental import pallas as pl
from jax.experimental.pallas import tpu as pltpu
from jax.sharding import PartitionSpec as P

W = 3072
YB = 384
TAPS = 4
TILTS = 32
ZD = 4
XP = 24
XQ = 128
NJ = 12
ROWS = YB // TILTS
PARTS = ((0, 8), (8, 4))
TILES = XP * ROWS // 16
HALF = YB // 2
QUARTER = YB // 4
DEPTH = 256
LEFT = 8
SPAN = 40
GROUP = 4

chi_scale = 200.0
phase_shift = 0.1
root_half = math.sqrt(0.5)
sin_third = math.sqrt(0.75)


def split_np(table):
    high = table.astype(ml_dtypes.bfloat16)
    low = (table - high.astype(np.float64)).astype(ml_dtypes.bfloat16)
    return high, low


def x_tables():
    n2 = np.arange(XQ)
    k2 = np.arange(XQ)
    forward = np.zeros((NJ, 2 * XQ, 2 * XQ))
    inverse = np.zeros((NJ, 2 * XQ, 2 * XQ))
    for j in range(NJ):
        if j == 0:
            for half, k1 in enumerate((0, 12)):
                angle = 2 * np.pi * ((n2[:, None] * (k1 + XP * k2[None, :])) % W) / W
                cas = np.cos(angle) + np.sin(angle)
                cut = slice(half * XQ, (half + 1) * XQ)
                forward[j, cut, cut] = cas
                inverse[j, cut, cut] = cas.T / W
        else:
            angle = 2 * np.pi * ((n2[:, None] * (j + XP * k2[None, :])) % W) / W
            cos, sin = np.cos(angle), np.sin(angle)
            forward[j] = np.block([[cos, -sin], [sin, cos]])
            inverse[j] = np.block([[cos.T, sin.T], [-sin.T, cos.T]]) * (2.0 / W)
    return forward, inverse


def x_frequencies():
    k2 = np.arange(XQ)
    result = np.zeros((NJ, 2 * XQ))
    for j in range(NJ):
        first, second = (0, 12) if j == 0 else (j, j)
        for half, k1 in enumerate((first, second)):
            k = k1 + XP * k2
            result[j, half * XQ : (half + 1) * XQ] = np.where(2 * k < W, k, k - W) / W
    return result


def y_frequencies():
    a = np.arange(YB)
    return np.where(2 * a < YB, a, a - YB) / YB


def y_tables():
    y = np.arange(HALF)
    wanted = np.array(
        [
            ROWS * d + first + i
            for first, count in PARTS
            for d in range(TILTS // 2)
            for i in range(count)
        ]
    )
    left, right = [], []
    for odd in range(2):
        a = np.arange(odd, YB, 2)

        def cas(rows):
            angle = 2 * np.pi * ((rows[:, None] * a[None, :]) % YB) / YB
            return np.cos(angle) + np.sin(angle)

        left.append(cas(wanted) / YB)
        given = cas(y).T
        swapped = np.concatenate([given[:, QUARTER:], given[:, :QUARTER]], axis=1)
        right.append([given, swapped])
    return np.array(left, np.float32), np.array(right, np.float32)


def real_eight(x):
    s0, d0 = x[0] + x[4], x[0] - x[4]
    s1, d1 = x[1] + x[5], x[1] - x[5]
    s2, d2 = x[2] + x[6], x[2] - x[6]
    s3, d3 = x[3] + x[7], x[3] - x[7]
    t0, t1 = s0 + s2, s1 + s3
    u = (d1 - d3) * root_half
    v = (d1 + d3) * root_half
    return {
        0: (t0 + t1, None),
        4: (t0 - t1, None),
        2: (s0 - s2, s3 - s1),
        1: (d0 + u, -(d2 + v)),
        3: (d0 - u, d2 - v),
    }


def forward_24(x):
    parts = [real_eight([x[(8 * a + 3 * b) % 24] for b in range(8)]) for a in range(3)]
    found = {}

    def put(ka, kb, value):
        for k in range(24):
            if k % 3 == ka % 3 and k % 8 == kb % 8:
                if k <= 12:
                    found[k] = value
                else:
                    re, im = value
                    found[24 - k] = (re, None if im is None else -im)

    for kb in (0, 4):
        p, q, r = (parts[a][kb][0] for a in range(3))
        total = q + r
        put(0, kb, (p + total, None))
        put(1, kb, (p - 0.5 * total, (r - q) * sin_third))
    for kb in (1, 2, 3):
        (pr, pi), (qr, qi), (rr, ri) = (parts[a][kb] for a in range(3))
        tr, ti = qr + rr, qi + ri
        put(0, kb, (pr + tr, pi + ti))
        mr, mi = pr - 0.5 * tr, pi - 0.5 * ti
        er, ei = (qr - rr) * sin_third, (qi - ri) * sin_third
        put(1, kb, (mr + ei, mi - er))
        put(2, kb, (mr - ei, mi + er))
    return found


def inverse_24(v):
    def get(ka, kb):
        k = next(i for i in range(24) if i % 3 == ka and i % 8 == kb)
        if k <= 12:
            return v[k]
        re, im = v[24 - k]
        return (re, -im)

    eights = [dict() for _ in range(3)]
    for kb in (0, 4):
        p = get(0, kb)[0]
        sr, si = get(1, kb)
        m = p - 0.5 * sr
        e = si * sin_third
        eights[0][kb] = (p + sr, None)
        eights[1][kb] = (m - e, None)
        eights[2][kb] = (m + e, None)
    for kb in (1, 2, 3):
        (pr, pi), (qr, qi), (rr, ri) = get(0, kb), get(1, kb), get(2, kb)
        tr, ti = qr + rr, qi + ri
        mr, mi = pr - 0.5 * tr, pi - 0.5 * ti
        er, ei = (qr - rr) * sin_third, (qi - ri) * sin_third
        eights[0][kb] = (pr + tr, pi + ti)
        eights[1][kb] = (mr - ei, mi + er)
        eights[2][kb] = (mr + ei, mi - er)
    out = [None] * 24
    for a in range(3):
        g = eights[a]
        g0, g4 = g[0][0], g[4][0]
        (r1, i1), (r2, i2), (r3, i3) = g[1], g[2], g[3]
        c0, c1 = g0 + g4, g0 - g4
        e0, e2 = c0 + r2, c0 - r2
        o0, o2 = r1 + r3, i1 - i3
        e1, e3 = c1 - i2, c1 + i2
        da, db = (r1 - r3) * root_half, (i1 + i3) * root_half
        o1, o3 = da - db, -(da + db)
        values = [e0 + o0, e1 + o1, e2 - o2, e3 + o3, e0 - o0, e1 - o1, e2 + o2, e3 - o3]
        for b in range(8):
            out[(8 * a + 3 * b) % 24] = values[b]
    return out


def split(value):
    high = value.astype(jnp.bfloat16)
    low = (value - high.astype(jnp.float32)).astype(jnp.bfloat16)
    return high, low


def three_products(high, low, table_high, table_low):
    left = jnp.concatenate([high, low, high], axis=1)
    right = jnp.concatenate([table_high, table_high, table_low], axis=0)
    return jnp.dot(left, right, preferred_element_type=jnp.float32)


STRIP = 16


def load_strips(x_refs, vh, vl, place=0):
    for n, x_ref in enumerate(x_refs, place):

        def strip(i, carry):
            rows = pl.ds(pl.multiple_of(i * STRIP, STRIP), STRIP)
            target = pl.ds(pl.multiple_of(n * QUARTER + i * STRIP, STRIP), STRIP)
            blocks = [
                x_ref[rows, b * XQ : (b + 1) * XQ].astype(jnp.float32) for b in range(XP)
            ]
            found = forward_24(blocks)
            for jj in range(NJ):
                if jj == 0:
                    pair = (found[0][0], found[12][0])
                else:
                    pair = found[jj]
                for half in range(2):
                    high, low = split(pair[half])
                    vh[jj, target, half * XQ : (half + 1) * XQ] = high
                    vl[jj, target, half * XQ : (half + 1) * XQ] = low
            return carry

        lax.fori_loop(0, QUARTER // STRIP, strip, 0)


def near_kernel(focus_ref, slab_ref, xa_ref, xb_ref, fh, fl, left_ref, right_ref, fy_ref, fx_ref,
                out_ref, mix_ref, gain_ref, vh, vl):
    load_strips((xa_ref, xb_ref), vh, vl)
    for j in range(NJ):
        out_ref[j] = three_products(vh[j], vl[j], fh[j], fl[j])
    scale = chi_scale * focus_ref[0]
    slab = slab_ref[0]
    angle_x = scale * (fx_ref[...] * fx_ref[...])
    cos_x, sin_x = jnp.cos(angle_x), jnp.sin(angle_x)
    for j in range(NJ):
        gain_ref[j] = jnp.concatenate([cos_x[j : j + 1], sin_x[j : j + 1]], axis=0)
    for odd in range(2):
        fy = fy_ref[odd : odd + 1, :]
        angle_y = scale * (fy * fy) + phase_shift
        left = left_ref[odd]
        side = jnp.concatenate([left * -jnp.sin(angle_y), left * -jnp.cos(angle_y)], axis=0)
        right = right_ref[odd, slab & 1]
        mixed = jnp.dot(
            side, right, precision=lax.Precision.HIGHEST, preferred_element_type=jnp.float32
        )
        if odd:
            mixed = mixed * jnp.where(slab < 2, 1.0, -1.0)
        empty = jnp.zeros((YB, DEPTH - HALF), jnp.float32)
        high, low = split(jnp.concatenate([mixed, empty], axis=1))
        mix_ref[odd] = jnp.concatenate([high, low, high], axis=1)


def parameters(megabytes):
    return pltpu.CompilerParams(vmem_limit_bytes=megabytes * 2**20)


def scalar_spec():
    return pl.BlockSpec(memory_space=pltpu.SMEM)


def vmem_spec():
    return pl.BlockSpec(memory_space=pltpu.VMEM)


def run_near(focus, slab, xa, xb, fh, fl):
    left, right = y_tables()
    fy = y_frequencies()
    fy = np.stack([fy[0::2], fy[1::2]]).astype(np.float32)
    fx = x_frequencies().astype(np.float32)
    return pl.pallas_call(
        near_kernel,
        in_specs=[scalar_spec()] * 2 + [vmem_spec()] * 8,
        out_specs=[vmem_spec()] * 3,
        out_shape=[
            jax.ShapeDtypeStruct((NJ, HALF, 2 * XQ), jnp.float32),
            jax.ShapeDtypeStruct((2, YB, 3 * DEPTH), jnp.bfloat16),
            jax.ShapeDtypeStruct((NJ, 2, 2 * XQ), jnp.float32),
        ],
        scratch_shapes=[pltpu.VMEM((NJ, HALF, 2 * XQ), jnp.bfloat16)] * 2,
        compiler_params=parameters(NEAR_MB),
        name="near",
    )(focus, slab, xa, xb, fh, fl, *(jnp.asarray(t) for t in (left, right, fy, fx)))


NEAR_MB = 24
MAIN_MB = 40
BAND_MB = 16
PROJECT_MB = 24


def main_kernel(xa, xb, near, mix, gain, fh, fl, ih, il, out, vh, vl, eh, el, oh, ol, zh, zl, back):
    load_strips((xa, xb), vh, vl)
    for j in range(NJ):
        far = three_products(vh[j], vl[j], fh[j], fl[j])
        here = near[j]
        eh[j], el[j] = split(here + far)
        oh[j], ol[j] = split(here - far)
    empty = jnp.zeros((DEPTH - HALF, 2 * XQ), jnp.bfloat16)
    for j in range(NJ):
        factors = gain[j]

        def mixed(odd, high, low):
            right = jnp.concatenate([high, empty, high, empty, low, empty], axis=0)
            y = jnp.dot(mix[odd], right, preferred_element_type=jnp.float32)
            return y[:HALF] * factors[0:1] + y[HALF:] * factors[1:2]

        even, odd = mixed(0, eh[j], el[j]), mixed(1, oh[j], ol[j])
        zh[j], zl[j] = split(jnp.concatenate([even + odd, even - odd], axis=0))
    for j in range(NJ):
        back[j] = three_products(zh[j], zl[j], ih[j], il[j])

    devices = TILTS // 2
    for half in range(2):
        low_row, low_tile = half * HALF, 0
        for _, count in PARTS:
            per_strip, per_tile = 8 // count, 16 // count

            def strip(i, carry):
                cut = pl.ds(pl.multiple_of(low_row + i * 8, 8), 8)
                v = {}
                for jj in range(NJ):
                    one, two = back[jj, cut, 0:XQ], back[jj, cut, XQ : 2 * XQ]
                    if jj == 0:
                        v[0], v[12] = (one, None), (two, None)
                    else:
                        v[jj] = (one, two)
                values = inverse_24(v)
                for part in range(per_strip):
                    some = slice(part * count, (part + 1) * count)
                    place = half * devices + i * per_strip + part
                    for tile in range(XP // per_tile):
                        joined = jnp.concatenate(
                            [values[per_tile * tile + n][some] for n in range(per_tile)], axis=0
                        )
                        out[place, low_tile + tile] = joined.astype(jnp.bfloat16)
                return carry

            lax.fori_loop(0, devices // per_strip, strip, 0)
            low_row += devices * count
            low_tile += XP // per_tile


def run_main(xa, xb, near, mix, gain, fh, fl, ih, il):
    args = (xa, xb, near, mix, gain, fh, fl, ih, il)
    half = pltpu.VMEM((NJ, HALF, 2 * XQ), jnp.bfloat16)
    full = pltpu.VMEM((NJ, YB, 2 * XQ), jnp.bfloat16)
    return pl.pallas_call(
        main_kernel,
        in_specs=[vmem_spec()] * len(args),
        out_specs=vmem_spec(),
        out_shape=jax.ShapeDtypeStruct((TILTS, TILES, 16, XQ), jnp.bfloat16),
        scratch_shapes=[half] * 6 + [full] * 2 + [pltpu.VMEM((NJ, YB, 2 * XQ), jnp.float32)],
        compiler_params=parameters(MAIN_MB),
        name="main",
    )(*args)


def band_kernel(off_ref, weight_ref, out_ref):
    distance = lax.broadcasted_iota(jnp.int32, (2 * XQ, XQ), 0) - lax.broadcasted_iota(
        jnp.int32, (2 * XQ, XQ), 1
    )
    distance = distance.astype(jnp.int16)

    def tilt(t, carry):
        for z in range(ZD):
            shift = off_ref[t, z] & (XQ - 1)
            band = jnp.zeros((2 * XQ, XQ), jnp.bfloat16)
            for tap in range(TAPS):
                weight = weight_ref[t, z * TAPS + tap].astype(jnp.bfloat16)
                band = jnp.where(distance == (shift + tap).astype(jnp.int16), weight, band)
            out_ref[t // GROUP, z, t % GROUP] = band
        return carry

    lax.fori_loop(0, TILTS, tilt, 0)


def run_band(off, weights):
    return pl.pallas_call(
        band_kernel,
        in_specs=[scalar_spec()] * 2,
        out_specs=vmem_spec(),
        out_shape=jax.ShapeDtypeStruct((TILTS // GROUP, ZD, GROUP, 2 * XQ, XQ), jnp.bfloat16),
        compiler_params=parameters(BAND_MB),
        name="bands",
    )(off, weights)


def project_kernel(off_ref, weight_ref, x, bands, out_ref, wide, narrow, total):
    wide[...] = jnp.zeros_like(wide)
    narrow[...] = jnp.zeros_like(narrow)
    total[...] = jnp.zeros_like(total)
    layouts = []
    base = 0
    for padded, (_, count) in zip((wide, narrow), PARTS):
        per_tile = 16 // count
        layouts.append((padded, count, per_tile, XP // per_tile, base))
        base += XP // per_tile

    def window(g, start):
        pieces = []
        for padded, count, per_tile, tiles, _ in layouts:
            log_tile = per_tile.bit_length() - 1
            piece = padded[start & (per_tile - 1), g, pl.ds(start >> log_tile, tiles)]
            pieces.append(piece.reshape(tiles * 16, XQ))
        return jnp.concatenate(pieces, axis=0)

    def step(i, carry):
        late = 0
        for g in range(GROUP):
            t = i * GROUP + g
            for z in range(ZD):
                late += jnp.where((off_ref[t, z] & (XQ - 1)) > XQ - TAPS + 1, 1, 0)
            for padded, count, per_tile, tiles, base in layouts:
                lead = LEFT // per_tile
                rows = [x[t, base + p].astype(jnp.float32) for p in range(tiles)]
                empty = jnp.zeros((16, XQ), jnp.float32)
                for p in range(tiles):
                    padded[0, g, lead + p] = x[t, base + p]
                for m in range(1, per_tile):
                    for p in range(-1, tiles):
                        here = rows[p] if p >= 0 else empty
                        later = rows[p + 1] if p + 1 < tiles else empty
                        tile = jnp.concatenate([here[m * count :], later[: m * count]], axis=0)
                        padded[m, g, lead + p] = tile.astype(jnp.bfloat16)
        for z in range(ZD):
            parts = []
            for g in range(GROUP):
                start = (off_ref[i * GROUP + g, z] >> 7) + LEFT
                parts.append(window(g, start))
                parts.append(window(g, start + 1))
            left = jnp.concatenate(parts, axis=1)
            band = bands[i, z].reshape(GROUP * 2 * XQ, XQ)
            total[z] += jnp.dot(left, band, preferred_element_type=jnp.float32)

        @pl.when(late > 0)
        def _():
            def pair(n, carry):
                g, z = n // ZD, n % ZD
                t = i * GROUP + g
                shift = off_ref[t, z] & (XQ - 1)

                @pl.when(shift > XQ - TAPS + 1)
                def _():
                    moved = (
                        lax.broadcasted_iota(jnp.int32, (XQ, XQ), 0)
                        - lax.broadcasted_iota(jnp.int32, (XQ, XQ), 1)
                        + (2 * XQ - shift)
                    )
                    band = jnp.zeros((XQ, XQ), jnp.float32)
                    for tap in range(TAPS):
                        band = jnp.where(moved == tap, weight_ref[t, z * TAPS + tap], band)
                    start = (off_ref[t, z] >> 7) + LEFT
                    total[z] += jnp.dot(
                        window(g, start + 2),
                        band.astype(jnp.bfloat16),
                        preferred_element_type=jnp.float32,
                    )

                return carry

            lax.fori_loop(0, GROUP * ZD, pair, 0)

        return carry

    lax.fori_loop(0, TILTS // GROUP, step, 0)
    for z in range(ZD):
        for (first, count), (_, _, _, _, base) in zip(PARTS, layouts):
            for b in range(XP):
                row = base * 16 + b * count
                out_ref[first : first + count, z, b * XQ : (b + 1) * XQ] = total[
                    z, row : row + count, :
                ]


def run_project(off, weights, moved, bands):
    return pl.pallas_call(
        project_kernel,
        in_specs=[scalar_spec()] * 2 + [vmem_spec()] * 2,
        out_specs=vmem_spec(),
        out_shape=jax.ShapeDtypeStruct((ROWS, ZD, W), jnp.float32),
        scratch_shapes=[
            pltpu.VMEM((2, GROUP, SPAN // 2, 16, XQ), jnp.bfloat16),
            pltpu.VMEM((4, GROUP, SPAN // 4, 16, XQ), jnp.bfloat16),
            pltpu.VMEM((ZD, TILES * 16, XQ), jnp.float32),
        ],
        compiler_params=parameters(PROJECT_MB),
        name="project",
    )(off, weights, moved, bands)


def body(tilts, tilt_defocus, defocus_table, slab_pick, interp_offset, interp_weights):
    def swap(block, bit):
        return lax.ppermute(block, "slab", [(i, i ^ bit) for i in range(4)])

    own = tilts[0]
    beside = swap(own, 1)
    across = swap(own, 2)
    entries = jnp.arange(defocus_table.shape[0], dtype=jnp.int32)
    group_defocus = jnp.sum(jnp.where(entries == slab_pick[0], defocus_table, 0.0))
    focus = tilt_defocus + group_defocus
    slab = lax.axis_index("slab").astype(jnp.int32).reshape(1)
    forward, inverse = x_tables()
    fh, fl = (jnp.asarray(t) for t in split_np(forward))
    ih, il = (jnp.asarray(t) for t in split_np(inverse))
    near, mix, gain = run_near(focus, slab, own, beside, fh, fl)
    near, across = lax.optimization_barrier((near, across))
    opposite = swap(across, 1)
    weights = interp_weights.astype(jnp.float32).reshape(TILTS, ZD * TAPS)
    bands = run_band(interp_offset, weights)
    filtered = run_main(across, opposite, near, mix, gain, fh, fl, ih, il)
    moved = lax.all_to_all(filtered, "dev", split_axis=0, concat_axis=0, tiled=True)
    return run_project(interp_offset, weights, moved, bands)


def solution(mesh):
    in_specs = (
        P("dev", "slab", None),
        P("dev"),
        P(),
        P("slab"),
        P(None, "slab"),
        P(None, "slab", None),
    )
    out_specs = P("dev", "slab", None)
    return jax.shard_map(body, mesh=mesh, in_specs=in_specs, out_specs=out_specs, check_vma=False)
```

```python
import math

import jax
import jax.numpy as jnp
import ml_dtypes
import numpy as np
from jax import lax
from jax.experimental import pallas as pl
from jax.experimental.pallas import tpu as pltpu
from jax.sharding import PartitionSpec as P

W = 3072
YB = 384
TAPS = 4
TILTS = 32
ZD = 4
XP = 24
XQ = 128
NJ = 12
ROWS = YB // TILTS
PARTS = ((0, 8), (8, 4))
TILES = XP * ROWS // 16
HALF = YB // 2
QUARTER = YB // 4
DEPTH = 256
LEFT = 8
SPAN = 40
GROUP = 4

chi_scale = 200.0
phase_shift = 0.1
root_half = math.sqrt(0.5)
sin_third = math.sqrt(0.75)


def split_np(table):
    high = table.astype(ml_dtypes.bfloat16)
    low = (table - high.astype(np.float64)).astype(ml_dtypes.bfloat16)
    return high, low


def x_table():
    n2 = np.arange(XQ)
    k2 = np.arange(XQ)
    table = np.zeros((NJ, 2 * XQ, 2 * XQ))
    for j in range(NJ):
        if j == 0:
            for half, k1 in enumerate((0, 12)):
                angle = 2 * np.pi * ((n2[:, None] * (k1 + XP * k2[None, :])) % W) / W
                cut = slice(half * XQ, (half + 1) * XQ)
                table[j, cut, cut] = np.cos(angle) + np.sin(angle)
        else:
            angle = 2 * np.pi * ((n2[:, None] * (j + XP * k2[None, :])) % W) / W
            cos, sin = np.cos(angle), np.sin(angle)
            table[j] = np.block([[cos, -sin], [sin, cos]])
    return table


def x_frequencies():
    k2 = np.arange(XQ)
    result = np.zeros((NJ, 2 * XQ))
    for j in range(NJ):
        first, second = (0, 12) if j == 0 else (j, j)
        for half, k1 in enumerate((first, second)):
            k = k1 + XP * k2
            result[j, half * XQ : (half + 1) * XQ] = np.where(2 * k < W, k, k - W) / W
    return result


def y_frequencies():
    a = np.arange(YB)
    return np.where(2 * a < YB, a, a - YB) / YB


def y_tables():
    y = np.arange(HALF)
    wanted = np.array(
        [
            ROWS * d + first + i
            for first, count in PARTS
            for d in range(TILTS // 2)
            for i in range(count)
        ]
    )
    left, right = [], []
    for odd in range(2):
        a = np.arange(odd, YB, 2)

        def cas(rows):
            angle = 2 * np.pi * ((rows[:, None] * a[None, :]) % YB) / YB
            return np.cos(angle) + np.sin(angle)

        left.append(cas(wanted) / YB)
        given = cas(y).T
        swapped = np.concatenate([given[:, QUARTER:], given[:, :QUARTER]], axis=1)
        right.append([given, swapped])
    return np.array(left, np.float32), np.array(right, np.float32)


def real_eight(x):
    s0, d0 = x[0] + x[4], x[0] - x[4]
    s1, d1 = x[1] + x[5], x[1] - x[5]
    s2, d2 = x[2] + x[6], x[2] - x[6]
    s3, d3 = x[3] + x[7], x[3] - x[7]
    t0, t1 = s0 + s2, s1 + s3
    u = (d1 - d3) * root_half
    v = (d1 + d3) * root_half
    return {
        0: (t0 + t1, None),
        4: (t0 - t1, None),
        2: (s0 - s2, s3 - s1),
        1: (d0 + u, -(d2 + v)),
        3: (d0 - u, d2 - v),
    }


def forward_24(x):
    parts = [real_eight([x[(8 * a + 3 * b) % 24] for b in range(8)]) for a in range(3)]
    found = {}

    def put(ka, kb, value):
        for k in range(24):
            if k % 3 == ka % 3 and k % 8 == kb % 8:
                if k <= 12:
                    found[k] = value
                else:
                    re, im = value
                    found[24 - k] = (re, None if im is None else -im)

    for kb in (0, 4):
        p, q, r = (parts[a][kb][0] for a in range(3))
        total = q + r
        put(0, kb, (p + total, None))
        put(1, kb, (p - 0.5 * total, (r - q) * sin_third))
    for kb in (1, 2, 3):
        (pr, pi), (qr, qi), (rr, ri) = (parts[a][kb] for a in range(3))
        tr, ti = qr + rr, qi + ri
        put(0, kb, (pr + tr, pi + ti))
        mr, mi = pr - 0.5 * tr, pi - 0.5 * ti
        er, ei = (qr - rr) * sin_third, (qi - ri) * sin_third
        put(1, kb, (mr + ei, mi - er))
        put(2, kb, (mr - ei, mi + er))
    return found


def inverse_24(v):
    def get(ka, kb):
        k = next(i for i in range(24) if i % 3 == ka and i % 8 == kb)
        if k <= 12:
            return v[k]
        re, im = v[24 - k]
        return (re, -im)

    eights = [dict() for _ in range(3)]
    for kb in (0, 4):
        p = get(0, kb)[0]
        sr, si = get(1, kb)
        m = p - 0.5 * sr
        e = si * sin_third
        eights[0][kb] = (p + sr, None)
        eights[1][kb] = (m - e, None)
        eights[2][kb] = (m + e, None)
    for kb in (1, 2, 3):
        (pr, pi), (qr, qi), (rr, ri) = get(0, kb), get(1, kb), get(2, kb)
        tr, ti = qr + rr, qi + ri
        mr, mi = pr - 0.5 * tr, pi - 0.5 * ti
        er, ei = (qr - rr) * sin_third, (qi - ri) * sin_third
        eights[0][kb] = (pr + tr, pi + ti)
        eights[1][kb] = (mr - ei, mi + er)
        eights[2][kb] = (mr + ei, mi - er)
    out = [None] * 24
    for a in range(3):
        g = eights[a]
        g0, g4 = g[0][0], g[4][0]
        (r1, i1), (r2, i2), (r3, i3) = g[1], g[2], g[3]
        c0, c1 = g0 + g4, g0 - g4
        e0, e2 = c0 + r2, c0 - r2
        o0, o2 = r1 + r3, i1 - i3
        e1, e3 = c1 - i2, c1 + i2
        da, db = (r1 - r3) * root_half, (i1 + i3) * root_half
        o1, o3 = da - db, -(da + db)
        values = [e0 + o0, e1 + o1, e2 - o2, e3 + o3, e0 - o0, e1 - o1, e2 + o2, e3 - o3]
        for b in range(8):
            out[(8 * a + 3 * b) % 24] = values[b]
    return out


def split(value):
    high = value.astype(jnp.bfloat16)
    low = (value - high.astype(jnp.float32)).astype(jnp.bfloat16)
    return high, low


def three_products(high, low, table_high, table_low):
    left = jnp.concatenate([high, low, high], axis=1)
    right = jnp.concatenate([table_high, table_high, table_low], axis=0)
    return jnp.dot(left, right, preferred_element_type=jnp.float32)


STRIP = 16


def load_strips(x_refs, vh, vl, place=0):
    for n, x_ref in enumerate(x_refs, place):

        def strip(i, carry):
            rows = pl.ds(pl.multiple_of(i * STRIP, STRIP), STRIP)
            target = pl.ds(pl.multiple_of(n * QUARTER + i * STRIP, STRIP), STRIP)
            blocks = [
                x_ref[rows, b * XQ : (b + 1) * XQ].astype(jnp.float32) for b in range(XP)
            ]
            found = forward_24(blocks)
            for jj in range(NJ):
                if jj == 0:
                    pair = (found[0][0], found[12][0])
                else:
                    pair = found[jj]
                for half in range(2):
                    high, low = split(pair[half])
                    vh[jj, target, half * XQ : (half + 1) * XQ] = high
                    vl[jj, target, half * XQ : (half + 1) * XQ] = low
            return carry

        lax.fori_loop(0, QUARTER // STRIP, strip, 0)


def near_kernel(focus_ref, slab_ref, xa_ref, xb_ref, fh, fl, left_ref, right_ref, fy_ref, fx_ref,
                out_ref, mix_ref, gain_ref, vh, vl):
    load_strips((xa_ref, xb_ref), vh, vl)
    for j in range(NJ):
        out_ref[j] = three_products(vh[j], vl[j], fh[j], fl[j])
    scale = chi_scale * focus_ref[0]
    slab = slab_ref[0]
    angle_x = scale * (fx_ref[...] * fx_ref[...])
    cos_x, sin_x = jnp.cos(angle_x), jnp.sin(angle_x)
    for j in range(NJ):
        scaled = jnp.concatenate([cos_x[j : j + 1], sin_x[j : j + 1]], axis=0)
        gain_ref[j] = scaled * ((1.0 if j == 0 else 2.0) / W)
    for odd in range(2):
        fy = fy_ref[odd : odd + 1, :]
        angle_y = scale * (fy * fy) + phase_shift
        left = left_ref[odd]
        side = jnp.concatenate([left * -jnp.sin(angle_y), left * -jnp.cos(angle_y)], axis=0)
        right = right_ref[odd, slab & 1]
        mixed = jnp.dot(
            side, right, precision=lax.Precision.HIGHEST, preferred_element_type=jnp.float32
        )
        if odd:
            mixed = mixed * jnp.where(slab < 2, 1.0, -1.0)
        empty = jnp.zeros((YB, DEPTH - HALF), jnp.float32)
        high, low = split(jnp.concatenate([mixed, empty], axis=1))
        mix_ref[odd] = jnp.concatenate([high, low, high], axis=1)


def parameters(megabytes):
    return pltpu.CompilerParams(vmem_limit_bytes=megabytes * 2**20)


def scalar_spec():
    return pl.BlockSpec(memory_space=pltpu.SMEM)


def vmem_spec():
    return pl.BlockSpec(memory_space=pltpu.VMEM)


def run_near(focus, slab, xa, xb, fh, fl):
    left, right = y_tables()
    fy = y_frequencies()
    fy = np.stack([fy[0::2], fy[1::2]]).astype(np.float32)
    fx = x_frequencies().astype(np.float32)
    return pl.pallas_call(
        near_kernel,
        in_specs=[scalar_spec()] * 2 + [vmem_spec()] * 8,
        out_specs=[vmem_spec()] * 3,
        out_shape=[
            jax.ShapeDtypeStruct((NJ, HALF, 2 * XQ), jnp.float32),
            jax.ShapeDtypeStruct((2, YB, 3 * DEPTH), jnp.bfloat16),
            jax.ShapeDtypeStruct((NJ, 2, 2 * XQ), jnp.float32),
        ],
        scratch_shapes=[pltpu.VMEM((NJ, HALF, 2 * XQ), jnp.bfloat16)] * 2,
        compiler_params=parameters(NEAR_MB),
        name="near",
    )(focus, slab, xa, xb, fh, fl, *(jnp.asarray(t) for t in (left, right, fy, fx)))


NEAR_MB = 24
MAIN_MB = 40
PROJECT_MB = 24


def quarter_kernel(x_ref, fh, fl, out_ref, vh, vl):
    load_strips((x_ref,), vh, vl)
    for j in range(NJ):
        out_ref[j] = three_products(vh[j], vl[j], fh[j], fl[j])


def run_quarter(x, fh, fl):
    return pl.pallas_call(
        quarter_kernel,
        in_specs=[vmem_spec()] * 3,
        out_specs=vmem_spec(),
        out_shape=jax.ShapeDtypeStruct((NJ, QUARTER, 2 * XQ), jnp.float32),
        scratch_shapes=[pltpu.VMEM((NJ, QUARTER, 2 * XQ), jnp.bfloat16)] * 2,
        compiler_params=parameters(NEAR_MB),
        name="quarter",
    )(x, fh, fl)


def main_kernel(xb, near, quarter, mix, gain, fh, fl, out, vh, vl, eh, el, oh, ol, zh, zl, back):
    load_strips((xb,), vh, vl)
    for j in range(NJ):
        last = three_products(vh[j], vl[j], fh[j], fl[j])
        far = jnp.concatenate([quarter[j], last], axis=0)
        here = near[j]
        eh[j], el[j] = split(here + far)
        oh[j], ol[j] = split(here - far)
    empty = jnp.zeros((DEPTH - HALF, 2 * XQ), jnp.bfloat16)
    for j in range(NJ):
        factors = gain[j]

        def mixed(odd, high, low):
            right = jnp.concatenate([high, empty, high, empty, low, empty], axis=0)
            y = jnp.dot(mix[odd], right, preferred_element_type=jnp.float32)
            return y[:HALF] * factors[0:1] + y[HALF:] * factors[1:2]

        even, odd = mixed(0, eh[j], el[j]), mixed(1, oh[j], ol[j])
        zh[j], zl[j] = split(jnp.concatenate([even + odd, even - odd], axis=0))
    for j in range(NJ):
        left = jnp.concatenate([zh[j], zl[j], zh[j]], axis=1)
        right = jnp.concatenate([fh[j], fh[j], fl[j]], axis=1)
        back[j] = lax.dot_general(
            left, right, (((1,), (1,)), ((), ())), preferred_element_type=jnp.float32
        )

    devices = TILTS // 2
    for half in range(2):
        low_row, low_tile = half * HALF, 0
        for _, count in PARTS:
            per_strip, per_tile = 8 // count, 16 // count

            def strip(i, carry):
                cut = pl.ds(pl.multiple_of(low_row + i * 8, 8), 8)
                v = {}
                for jj in range(NJ):
                    one, two = back[jj, cut, 0:XQ], back[jj, cut, XQ : 2 * XQ]
                    if jj == 0:
                        v[0], v[12] = (one, None), (two, None)
                    else:
                        v[jj] = (one, two)
                values = inverse_24(v)
                for part in range(per_strip):
                    some = slice(part * count, (part + 1) * count)
                    place = half * devices + i * per_strip + part
                    for tile in range(XP // per_tile):
                        joined = jnp.concatenate(
                            [values[per_tile * tile + n][some] for n in range(per_tile)], axis=0
                        )
                        out[place, low_tile + tile] = joined.astype(jnp.bfloat16)
                return carry

            lax.fori_loop(0, devices // per_strip, strip, 0, unroll=4)
            low_row += devices * count
            low_tile += XP // per_tile


def run_main(xb, near, quarter, mix, gain, fh, fl):
    args = (xb, near, quarter, mix, gain, fh, fl)
    fourth = pltpu.VMEM((NJ, QUARTER, 2 * XQ), jnp.bfloat16)
    half = pltpu.VMEM((NJ, HALF, 2 * XQ), jnp.bfloat16)
    full = pltpu.VMEM((NJ, YB, 2 * XQ), jnp.bfloat16)
    return pl.pallas_call(
        main_kernel,
        in_specs=[vmem_spec()] * len(args),
        out_specs=vmem_spec(),
        out_shape=jax.ShapeDtypeStruct((TILTS, TILES, 16, XQ), jnp.bfloat16),
        scratch_shapes=[fourth] * 2 + [half] * 4 + [full] * 2 + [pltpu.VMEM((NJ, YB, 2 * XQ), jnp.float32)],
        compiler_params=parameters(MAIN_MB),
        name="main",
    )(*args)


def project_kernel(off_ref, weight_ref, x, out_ref, wide, narrow, total):
    wide[...] = jnp.zeros_like(wide)
    narrow[...] = jnp.zeros_like(narrow)
    total[...] = jnp.zeros_like(total)
    layouts = []
    base = 0
    for padded, (_, count) in zip((wide, narrow), PARTS):
        per_tile = 16 // count
        layouts.append((padded, count, per_tile, XP // per_tile, base))
        base += XP // per_tile

    def window(g, start):
        pieces = []
        for padded, count, per_tile, tiles, _ in layouts:
            log_tile = per_tile.bit_length() - 1
            piece = padded[start & (per_tile - 1), g, pl.ds(start >> log_tile, tiles)]
            pieces.append(piece.reshape(tiles * 16, XQ))
        return jnp.concatenate(pieces, axis=0)

    distance = lax.broadcasted_iota(jnp.int32, (2 * XQ, XQ), 0) - lax.broadcasted_iota(
        jnp.int32, (2 * XQ, XQ), 1
    )
    distance = distance.astype(jnp.int16)

    def band_of(t, z):
        shift = off_ref[t, z] & (XQ - 1)
        band = jnp.zeros((2 * XQ, XQ), jnp.bfloat16)
        for tap in range(TAPS):
            weight = weight_ref[t, z * TAPS + tap].astype(jnp.bfloat16)
            band = jnp.where(distance == (shift + tap).astype(jnp.int16), weight, band)
        return band

    def step(i, carry):
        late = 0
        for g in range(GROUP):
            t = i * GROUP + g
            for z in range(ZD):
                late += jnp.where((off_ref[t, z] & (XQ - 1)) > XQ - TAPS + 1, 1, 0)
            for padded, count, per_tile, tiles, base in layouts:
                lead = LEFT // per_tile
                rows = [x[t, base + p].astype(jnp.float32) for p in range(tiles)]
                empty = jnp.zeros((16, XQ), jnp.float32)
                for p in range(tiles):
                    padded[0, g, lead + p] = x[t, base + p]
                for m in range(1, per_tile):
                    for p in range(-1, tiles):
                        here = rows[p] if p >= 0 else empty
                        later = rows[p + 1] if p + 1 < tiles else empty
                        tile = jnp.concatenate([here[m * count :], later[: m * count]], axis=0)
                        padded[m, g, lead + p] = tile.astype(jnp.bfloat16)
        for z in range(ZD):
            parts = []
            for g in range(GROUP):
                start = (off_ref[i * GROUP + g, z] >> 7) + LEFT
                parts.append(window(g, start))
                parts.append(window(g, start + 1))
            left = jnp.concatenate(parts, axis=1)
            band = jnp.concatenate([band_of(i * GROUP + g, z) for g in range(GROUP)], axis=0)
            total[z] += jnp.dot(left, band, preferred_element_type=jnp.float32)

        @pl.when(late > 0)
        def _():
            def pair(n, carry):
                g, z = n // ZD, n % ZD
                t = i * GROUP + g
                shift = off_ref[t, z] & (XQ - 1)

                @pl.when(shift > XQ - TAPS + 1)
                def _():
                    moved = (
                        lax.broadcasted_iota(jnp.int32, (XQ, XQ), 0)
                        - lax.broadcasted_iota(jnp.int32, (XQ, XQ), 1)
                        + (2 * XQ - shift)
                    )
                    band = jnp.zeros((XQ, XQ), jnp.float32)
                    for tap in range(TAPS):
                        band = jnp.where(moved == tap, weight_ref[t, z * TAPS + tap], band)
                    start = (off_ref[t, z] >> 7) + LEFT
                    total[z] += jnp.dot(
                        window(g, start + 2),
                        band.astype(jnp.bfloat16),
                        preferred_element_type=jnp.float32,
                    )

                return carry

            lax.fori_loop(0, GROUP * ZD, pair, 0)

        return carry

    lax.fori_loop(0, TILTS // GROUP, step, 0)
    for z in range(ZD):
        for (first, count), (_, _, _, _, base) in zip(PARTS, layouts):
            for b in range(XP):
                row = base * 16 + b * count
                out_ref[first : first + count, z, b * XQ : (b + 1) * XQ] = total[
                    z, row : row + count, :
                ]


def run_project(off, weights, moved):
    return pl.pallas_call(
        project_kernel,
        in_specs=[scalar_spec()] * 2 + [vmem_spec()],
        out_specs=vmem_spec(),
        out_shape=jax.ShapeDtypeStruct((ROWS, ZD, W), jnp.float32),
        scratch_shapes=[
            pltpu.VMEM((2, GROUP, SPAN // 2, 16, XQ), jnp.bfloat16),
            pltpu.VMEM((4, GROUP, SPAN // 4, 16, XQ), jnp.bfloat16),
            pltpu.VMEM((ZD, TILES * 16, XQ), jnp.float32),
        ],
        compiler_params=parameters(PROJECT_MB),
        name="project",
    )(off, weights, moved)


def body(tilts, tilt_defocus, defocus_table, slab_pick, interp_offset, interp_weights):
    def swap(block, bit):
        return lax.ppermute(block, "slab", [(i, i ^ bit) for i in range(4)])

    own = tilts[0]
    beside = swap(own, 1)
    across = swap(own, 2)
    entries = jnp.arange(defocus_table.shape[0], dtype=jnp.int32)
    group_defocus = jnp.sum(jnp.where(entries == slab_pick[0], defocus_table, 0.0))
    focus = tilt_defocus + group_defocus
    slab = lax.axis_index("slab").astype(jnp.int32).reshape(1)
    fh, fl = (jnp.asarray(t) for t in split_np(x_table()))
    near, mix, gain = run_near(focus, slab, own, beside, fh, fl)
    near, across = lax.optimization_barrier((near, across))
    opposite = swap(across, 1)
    weights = interp_weights.astype(jnp.float32).reshape(TILTS, ZD * TAPS)
    quarter = run_quarter(across, fh, fl)
    quarter, opposite = lax.optimization_barrier((quarter, opposite))
    filtered = run_main(opposite, near, quarter, mix, gain, fh, fl)
    moved = lax.all_to_all(filtered, "dev", split_axis=0, concat_axis=0, tiled=True)
    return run_project(interp_offset, weights, moved)


def solution(mesh):
    in_specs = (
        P("dev", "slab", None),
        P("dev"),
        P(),
        P("slab"),
        P(None, "slab"),
        P(None, "slab", None),
    )
    out_specs = P("dev", "slab", None)
    return jax.shard_map(body, mesh=mesh, in_specs=in_specs, out_specs=out_specs, check_vma=False)
```

```python
import math

import jax
import jax.numpy as jnp
import ml_dtypes
import numpy as np
from jax import lax
from jax.experimental import pallas as pl
from jax.experimental.pallas import tpu as pltpu
from jax.sharding import PartitionSpec as P

W = 3072
YB = 384
TAPS = 4
TILTS = 32
ZD = 4
XP = 24
XQ = 128
NJ = 12
ROWS = YB // TILTS
PARTS = ((0, 8), (8, 4))
TILES = XP * ROWS // 16
HALF = YB // 2
QUARTER = YB // 4
DEPTH = 256
LEFT = 8
SPAN = 40
GROUP = 4

chi_scale = 200.0
phase_shift = 0.1
root_half = math.sqrt(0.5)
sin_third = math.sqrt(0.75)


def split_np(table):
    high = table.astype(ml_dtypes.bfloat16)
    low = (table - high.astype(np.float64)).astype(ml_dtypes.bfloat16)
    return high, low


def x_table():
    n2 = np.arange(XQ)
    k2 = np.arange(XQ)
    table = np.zeros((NJ, 2 * XQ, 2 * XQ))
    for j in range(NJ):
        if j == 0:
            for half, k1 in enumerate((0, 12)):
                angle = 2 * np.pi * ((n2[:, None] * (k1 + XP * k2[None, :])) % W) / W
                cut = slice(half * XQ, (half + 1) * XQ)
                table[j, cut, cut] = np.cos(angle) + np.sin(angle)
        else:
            angle = 2 * np.pi * ((n2[:, None] * (j + XP * k2[None, :])) % W) / W
            cos, sin = np.cos(angle), np.sin(angle)
            table[j] = np.block([[cos, -sin], [sin, cos]])
    return table


def frequency(index, count):
    return jnp.where(2 * index < count, index, index - count).astype(jnp.float32) / count


def x_frequencies():
    shape = (NJ, 2 * XQ)
    j = lax.broadcasted_iota(jnp.int32, shape, 0)
    place = lax.broadcasted_iota(jnp.int32, shape, 1)
    k1 = jnp.where(j == 0, jnp.where(place < XQ, 0, XP // 2), j)
    return frequency(k1 + XP * (place & (XQ - 1)), W)


def y_frequencies(odd):
    return frequency(2 * lax.broadcasted_iota(jnp.int32, (1, HALF), 1) + odd, YB)


def y_tables():
    y = np.arange(HALF)
    wanted = np.array(
        [
            ROWS * d + first + i
            for first, count in PARTS
            for d in range(TILTS // 2)
            for i in range(count)
        ]
    )
    left, right = [], []
    for odd in range(2):
        a = np.arange(odd, YB, 2)

        def cas(rows):
            angle = 2 * np.pi * ((rows[:, None] * a[None, :]) % YB) / YB
            return np.cos(angle) + np.sin(angle)

        left.append(cas(wanted) / YB)
        given = cas(y).T
        swapped = np.concatenate([given[:, QUARTER:], given[:, :QUARTER]], axis=1)
        right.append([given, swapped])
    return np.array(left, np.float32), np.array(right, np.float32)


def real_eight(x):
    s0, d0 = x[0] + x[4], x[0] - x[4]
    s1, d1 = x[1] + x[5], x[1] - x[5]
    s2, d2 = x[2] + x[6], x[2] - x[6]
    s3, d3 = x[3] + x[7], x[3] - x[7]
    t0, t1 = s0 + s2, s1 + s3
    u = (d1 - d3) * root_half
    v = (d1 + d3) * root_half
    return {
        0: (t0 + t1, None),
        4: (t0 - t1, None),
        2: (s0 - s2, s3 - s1),
        1: (d0 + u, -(d2 + v)),
        3: (d0 - u, d2 - v),
    }


def forward_24(x):
    parts = [real_eight([x[(8 * a + 3 * b) % 24] for b in range(8)]) for a in range(3)]
    found = {}

    def put(ka, kb, value):
        for k in range(24):
            if k % 3 == ka % 3 and k % 8 == kb % 8:
                if k <= 12:
                    found[k] = value
                else:
                    re, im = value
                    found[24 - k] = (re, None if im is None else -im)

    for kb in (0, 4):
        p, q, r = (parts[a][kb][0] for a in range(3))
        total = q + r
        put(0, kb, (p + total, None))
        put(1, kb, (p - 0.5 * total, (r - q) * sin_third))
    for kb in (1, 2, 3):
        (pr, pi), (qr, qi), (rr, ri) = (parts[a][kb] for a in range(3))
        tr, ti = qr + rr, qi + ri
        put(0, kb, (pr + tr, pi + ti))
        mr, mi = pr - 0.5 * tr, pi - 0.5 * ti
        er, ei = (qr - rr) * sin_third, (qi - ri) * sin_third
        put(1, kb, (mr + ei, mi - er))
        put(2, kb, (mr - ei, mi + er))
    return found


def inverse_24(v):
    def get(ka, kb):
        k = next(i for i in range(24) if i % 3 == ka and i % 8 == kb)
        if k <= 12:
            return v[k]
        re, im = v[24 - k]
        return (re, -im)

    eights = [dict() for _ in range(3)]
    for kb in (0, 4):
        p = get(0, kb)[0]
        sr, si = get(1, kb)
        m = p - 0.5 * sr
        e = si * sin_third
        eights[0][kb] = (p + sr, None)
        eights[1][kb] = (m - e, None)
        eights[2][kb] = (m + e, None)
    for kb in (1, 2, 3):
        (pr, pi), (qr, qi), (rr, ri) = get(0, kb), get(1, kb), get(2, kb)
        tr, ti = qr + rr, qi + ri
        mr, mi = pr - 0.5 * tr, pi - 0.5 * ti
        er, ei = (qr - rr) * sin_third, (qi - ri) * sin_third
        eights[0][kb] = (pr + tr, pi + ti)
        eights[1][kb] = (mr - ei, mi + er)
        eights[2][kb] = (mr + ei, mi - er)
    out = [None] * 24
    for a in range(3):
        g = eights[a]
        g0, g4 = g[0][0], g[4][0]
        (r1, i1), (r2, i2), (r3, i3) = g[1], g[2], g[3]
        c0, c1 = g0 + g4, g0 - g4
        e0, e2 = c0 + r2, c0 - r2
        o0, o2 = r1 + r3, i1 - i3
        e1, e3 = c1 - i2, c1 + i2
        da, db = (r1 - r3) * root_half, (i1 + i3) * root_half
        o1, o3 = da - db, -(da + db)
        values = [e0 + o0, e1 + o1, e2 - o2, e3 + o3, e0 - o0, e1 - o1, e2 + o2, e3 - o3]
        for b in range(8):
            out[(8 * a + 3 * b) % 24] = values[b]
    return out


def split(value):
    high = value.astype(jnp.bfloat16)
    low = (value - high.astype(jnp.float32)).astype(jnp.bfloat16)
    return high, low


def three_products(high, low, table_high, table_low):
    left = jnp.concatenate([high, low, high], axis=1)
    right = jnp.concatenate([table_high, table_high, table_low], axis=0)
    return jnp.dot(left, right, preferred_element_type=jnp.float32)


STRIP = 16


def load_strips(x_refs, vh, vl, place=0):
    for n, x_ref in enumerate(x_refs, place):

        def strip(i, carry):
            rows = pl.ds(pl.multiple_of(i * STRIP, STRIP), STRIP)
            target = pl.ds(pl.multiple_of(n * QUARTER + i * STRIP, STRIP), STRIP)
            blocks = [
                x_ref[rows, b * XQ : (b + 1) * XQ].astype(jnp.float32) for b in range(XP)
            ]
            found = forward_24(blocks)
            for jj in range(NJ):
                if jj == 0:
                    pair = (found[0][0], found[12][0])
                else:
                    pair = found[jj]
                for half in range(2):
                    high, low = split(pair[half])
                    vh[jj, target, half * XQ : (half + 1) * XQ] = high
                    vl[jj, target, half * XQ : (half + 1) * XQ] = low
            return carry

        lax.fori_loop(0, QUARTER // STRIP, strip, 0)


def near_kernel(focus_ref, slab_ref, xa_ref, xb_ref, fh, fl, left_ref, right_ref, out_ref, mix_ref,
                gain_ref, vh, vl):
    load_strips((xa_ref, xb_ref), vh, vl)
    for j in range(NJ):
        out_ref[j] = three_products(vh[j], vl[j], fh[j], fl[j])
    scale = chi_scale * focus_ref[0]
    slab = slab_ref[0]
    fx = x_frequencies()
    angle_x = scale * (fx * fx)
    cos_x, sin_x = jnp.cos(angle_x), jnp.sin(angle_x)
    for j in range(NJ):
        scaled = jnp.concatenate([cos_x[j : j + 1], sin_x[j : j + 1]], axis=0)
        gain_ref[j] = scaled * ((1.0 if j == 0 else 2.0) / W)
    for odd in range(2):
        fy = y_frequencies(odd)
        angle_y = scale * (fy * fy) + phase_shift
        left = left_ref[odd]
        side = jnp.concatenate([left * -jnp.sin(angle_y), left * -jnp.cos(angle_y)], axis=0)
        right = right_ref[odd, slab & 1]
        mixed = jnp.dot(
            side, right, precision=lax.Precision.HIGHEST, preferred_element_type=jnp.float32
        )
        if odd:
            mixed = mixed * jnp.where(slab < 2, 1.0, -1.0)
        empty = jnp.zeros((YB, DEPTH - HALF), jnp.float32)
        high, low = split(jnp.concatenate([mixed, empty], axis=1))
        mix_ref[odd] = jnp.concatenate([high, low, high], axis=1)


def parameters(megabytes):
    return pltpu.CompilerParams(vmem_limit_bytes=megabytes * 2**20)


def scalar_spec():
    return pl.BlockSpec(memory_space=pltpu.SMEM)


def vmem_spec():
    return pl.BlockSpec(memory_space=pltpu.VMEM)


def run_near(focus, slab, xa, xb, fh, fl):
    left, right = y_tables()
    return pl.pallas_call(
        near_kernel,
        in_specs=[scalar_spec()] * 2 + [vmem_spec()] * 6,
        out_specs=[vmem_spec()] * 3,
        out_shape=[
            jax.ShapeDtypeStruct((NJ, HALF, 2 * XQ), jnp.float32),
            jax.ShapeDtypeStruct((2, YB, 3 * DEPTH), jnp.bfloat16),
            jax.ShapeDtypeStruct((NJ, 2, 2 * XQ), jnp.float32),
        ],
        scratch_shapes=[pltpu.VMEM((NJ, HALF, 2 * XQ), jnp.bfloat16)] * 2,
        compiler_params=parameters(NEAR_MB),
        name="near",
    )(focus, slab, xa, xb, fh, fl, jnp.asarray(left), jnp.asarray(right))


NEAR_MB = 24
MAIN_MB = 40
PROJECT_MB = 24


def quarter_kernel(x_ref, fh, fl, out_ref, vh, vl):
    load_strips((x_ref,), vh, vl)
    for j in range(NJ):
        out_ref[j] = three_products(vh[j], vl[j], fh[j], fl[j])


def run_quarter(x, fh, fl):
    return pl.pallas_call(
        quarter_kernel,
        in_specs=[vmem_spec()] * 3,
        out_specs=vmem_spec(),
        out_shape=jax.ShapeDtypeStruct((NJ, QUARTER, 2 * XQ), jnp.float32),
        scratch_shapes=[pltpu.VMEM((NJ, QUARTER, 2 * XQ), jnp.bfloat16)] * 2,
        compiler_params=parameters(NEAR_MB),
        name="quarter",
    )(x, fh, fl)


def main_kernel(xb, near, quarter, mix, gain, fh, fl, ih, il, out, vh, vl, eh, el, oh, ol, zh, zl, back):
    load_strips((xb,), vh, vl)
    for j in range(NJ):
        last = three_products(vh[j], vl[j], fh[j], fl[j])
        far = jnp.concatenate([quarter[j], last], axis=0)
        here = near[j]
        eh[j], el[j] = split(here + far)
        oh[j], ol[j] = split(here - far)
    empty = jnp.zeros((DEPTH - HALF, 2 * XQ), jnp.bfloat16)
    for j in range(NJ):
        factors = gain[j]

        def mixed(odd, high, low):
            right = jnp.concatenate([high, empty, high, empty, low, empty], axis=0)
            y = jnp.dot(mix[odd], right, preferred_element_type=jnp.float32)
            return y[:HALF] * factors[0:1] + y[HALF:] * factors[1:2]

        even, odd = mixed(0, eh[j], el[j]), mixed(1, oh[j], ol[j])
        zh[j], zl[j] = split(jnp.concatenate([even + odd, even - odd], axis=0))
    for j in range(NJ):
        left = jnp.concatenate([zh[j], zl[j], zh[j]], axis=1)
        right = jnp.concatenate([ih[j], ih[j], il[j]], axis=0)
        back[j] = jnp.dot(left, right, preferred_element_type=jnp.float32)

    devices = TILTS // 2
    for half in range(2):
        low_row, low_tile = half * HALF, 0
        for _, count in PARTS:
            per_strip, per_tile = 8 // count, 16 // count

            def strip(i, carry):
                cut = pl.ds(pl.multiple_of(low_row + i * 8, 8), 8)
                v = {}
                for jj in range(NJ):
                    one, two = back[jj, cut, 0:XQ], back[jj, cut, XQ : 2 * XQ]
                    if jj == 0:
                        v[0], v[12] = (one, None), (two, None)
                    else:
                        v[jj] = (one, two)
                values = inverse_24(v)
                for part in range(per_strip):
                    some = slice(part * count, (part + 1) * count)
                    place = half * devices + i * per_strip + part
                    for tile in range(XP // per_tile):
                        joined = jnp.concatenate(
                            [values[per_tile * tile + n][some] for n in range(per_tile)], axis=0
                        )
                        out[place, low_tile + tile] = joined.astype(jnp.bfloat16)
                return carry

            lax.fori_loop(0, devices // per_strip, strip, 0, unroll=4)
            low_row += devices * count
            low_tile += XP // per_tile


def run_main(xb, near, quarter, mix, gain, fh, fl, ih, il):
    args = (xb, near, quarter, mix, gain, fh, fl, ih, il)
    fourth = pltpu.VMEM((NJ, QUARTER, 2 * XQ), jnp.bfloat16)
    half = pltpu.VMEM((NJ, HALF, 2 * XQ), jnp.bfloat16)
    full = pltpu.VMEM((NJ, YB, 2 * XQ), jnp.bfloat16)
    return pl.pallas_call(
        main_kernel,
        in_specs=[vmem_spec()] * len(args),
        out_specs=vmem_spec(),
        out_shape=jax.ShapeDtypeStruct((TILTS, TILES, 16, XQ), jnp.bfloat16),
        scratch_shapes=[fourth] * 2 + [half] * 4 + [full] * 2 + [pltpu.VMEM((NJ, YB, 2 * XQ), jnp.float32)],
        compiler_params=parameters(MAIN_MB),
        name="main",
    )(*args)


def project_kernel(off_ref, weight_ref, x, out_ref, wide, narrow, total):
    wide[...] = jnp.zeros_like(wide)
    narrow[...] = jnp.zeros_like(narrow)
    total[...] = jnp.zeros_like(total)
    layouts = []
    base = 0
    for padded, (_, count) in zip((wide, narrow), PARTS):
        per_tile = 16 // count
        layouts.append((padded, count, per_tile, XP // per_tile, base))
        base += XP // per_tile

    def window(g, start):
        pieces = []
        for padded, count, per_tile, tiles, _ in layouts:
            log_tile = per_tile.bit_length() - 1
            piece = padded[start & (per_tile - 1), g, pl.ds(start >> log_tile, tiles)]
            pieces.append(piece.reshape(tiles * 16, XQ))
        return jnp.concatenate(pieces, axis=0)

    distance = lax.broadcasted_iota(jnp.int32, (2 * XQ, XQ), 0) - lax.broadcasted_iota(
        jnp.int32, (2 * XQ, XQ), 1
    )
    distance = distance.astype(jnp.int16)

    def band_of(t, z):
        shift = off_ref[t, z] & (XQ - 1)
        band = jnp.zeros((2 * XQ, XQ), jnp.bfloat16)
        for tap in range(TAPS):
            weight = weight_ref[t, z * TAPS + tap].astype(jnp.bfloat16)
            band = jnp.where(distance == (shift + tap).astype(jnp.int16), weight, band)
        return band

    def step(i, carry):
        late = 0
        for g in range(GROUP):
            t = i * GROUP + g
            for z in range(ZD):
                late += jnp.where((off_ref[t, z] & (XQ - 1)) > XQ - TAPS + 1, 1, 0)
            for padded, count, per_tile, tiles, base in layouts:
                lead = LEFT // per_tile
                rows = [x[t, base + p].astype(jnp.float32) for p in range(tiles)]
                empty = jnp.zeros((16, XQ), jnp.float32)
                for p in range(tiles):
                    padded[0, g, lead + p] = x[t, base + p]
                for m in range(1, per_tile):
                    for p in range(-1, tiles):
                        here = rows[p] if p >= 0 else empty
                        later = rows[p + 1] if p + 1 < tiles else empty
                        tile = jnp.concatenate([here[m * count :], later[: m * count]], axis=0)
                        padded[m, g, lead + p] = tile.astype(jnp.bfloat16)
        for z in range(ZD):
            parts = []
            for g in range(GROUP):
                start = (off_ref[i * GROUP + g, z] >> 7) + LEFT
                parts.append(window(g, start))
                parts.append(window(g, start + 1))
            left = jnp.concatenate(parts, axis=1)
            band = jnp.concatenate([band_of(i * GROUP + g, z) for g in range(GROUP)], axis=0)
            total[z] += jnp.dot(left, band, preferred_element_type=jnp.float32)

        @pl.when(late > 0)
        def _():
            def pair(n, carry):
                g, z = n // ZD, n % ZD
                t = i * GROUP + g
                shift = off_ref[t, z] & (XQ - 1)

                @pl.when(shift > XQ - TAPS + 1)
                def _():
                    moved = (
                        lax.broadcasted_iota(jnp.int32, (XQ, XQ), 0)
                        - lax.broadcasted_iota(jnp.int32, (XQ, XQ), 1)
                        + (2 * XQ - shift)
                    )
                    band = jnp.zeros((XQ, XQ), jnp.float32)
                    for tap in range(TAPS):
                        band = jnp.where(moved == tap, weight_ref[t, z * TAPS + tap], band)
                    start = (off_ref[t, z] >> 7) + LEFT
                    total[z] += jnp.dot(
                        window(g, start + 2),
                        band.astype(jnp.bfloat16),
                        preferred_element_type=jnp.float32,
                    )

                return carry

            lax.fori_loop(0, GROUP * ZD, pair, 0)

        return carry

    lax.fori_loop(0, TILTS // GROUP, step, 0)
    for z in range(ZD):
        for (first, count), (_, _, _, _, base) in zip(PARTS, layouts):
            for b in range(XP):
                row = base * 16 + b * count
                out_ref[first : first + count, z, b * XQ : (b + 1) * XQ] = total[
                    z, row : row + count, :
                ]


def run_project(off, weights, moved):
    return pl.pallas_call(
        project_kernel,
        in_specs=[scalar_spec()] * 2 + [vmem_spec()],
        out_specs=vmem_spec(),
        out_shape=jax.ShapeDtypeStruct((ROWS, ZD, W), jnp.float32),
        scratch_shapes=[
            pltpu.VMEM((2, GROUP, SPAN // 2, 16, XQ), jnp.bfloat16),
            pltpu.VMEM((4, GROUP, SPAN // 4, 16, XQ), jnp.bfloat16),
            pltpu.VMEM((ZD, TILES * 16, XQ), jnp.float32),
        ],
        compiler_params=parameters(PROJECT_MB),
        name="project",
    )(off, weights, moved)


def body(tilts, tilt_defocus, defocus_table, slab_pick, interp_offset, interp_weights):
    def swap(block, bit):
        return lax.ppermute(block, "slab", [(i, i ^ bit) for i in range(4)])

    own = tilts[0]
    across = swap(own, 2)
    beside = swap(own, 1)
    entries = jnp.arange(defocus_table.shape[0], dtype=jnp.int32)
    group_defocus = jnp.sum(jnp.where(entries == slab_pick[0], defocus_table, 0.0))
    focus = tilt_defocus + group_defocus
    slab = lax.axis_index("slab").astype(jnp.int32).reshape(1)
    fh, fl = (jnp.asarray(t) for t in split_np(x_table()))
    ih, il = (jnp.asarray(t) for t in split_np(np.swapaxes(x_table(), 1, 2)))
    near, mix, gain = run_near(focus, slab, own, beside, fh, fl)
    near, across = lax.optimization_barrier((near, across))
    opposite = swap(across, 1)
    weights = interp_weights.astype(jnp.float32).reshape(TILTS, ZD * TAPS)
    quarter = run_quarter(across, fh, fl)
    quarter, opposite = lax.optimization_barrier((quarter, opposite))
    filtered = run_main(opposite, near, quarter, mix, gain, fh, fl, ih, il)
    moved = lax.all_to_all(filtered, "dev", split_axis=0, concat_axis=0, tiled=True)
    return run_project(interp_offset, weights, moved)


def solution(mesh):
    in_specs = (
        P("dev", "slab", None),
        P("dev"),
        P(),
        P("slab"),
        P(None, "slab"),
        P(None, "slab", None),
    )
    out_specs = P("dev", "slab", None)
    return jax.shard_map(body, mesh=mesh, in_specs=in_specs, out_specs=out_specs, check_vma=False)
```

```python
import math

import jax
import jax.numpy as jnp
import ml_dtypes
import numpy as np
from jax import lax
from jax.experimental import pallas as pl
from jax.experimental.pallas import tpu as pltpu
from jax.sharding import PartitionSpec as P

W = 3072
YB = 384
TAPS = 4
TILTS = 32
ZD = 4
XP = 24
XQ = 128
NJ = 12
ROWS = YB // TILTS
PARTS = ((0, 8), (8, 4))
TILES = XP * ROWS // 16
HALF = YB // 2
QUARTER = YB // 4
DEPTH = 256
LEFT = 8
SPAN = 40
GROUP = 4

chi_scale = 200.0
phase_shift = 0.1
root_half = math.sqrt(0.5)
sin_third = math.sqrt(0.75)


def split_np(table):
    high = table.astype(ml_dtypes.bfloat16)
    low = (table - high.astype(np.float64)).astype(ml_dtypes.bfloat16)
    return high, low


def x_table():
    n2 = np.arange(XQ)
    k2 = np.arange(XQ)
    table = np.zeros((NJ, 2 * XQ, 2 * XQ))
    for j in range(NJ):
        if j == 0:
            for half, k1 in enumerate((0, 12)):
                angle = 2 * np.pi * ((n2[:, None] * (k1 + XP * k2[None, :])) % W) / W
                cut = slice(half * XQ, (half + 1) * XQ)
                table[j, cut, cut] = np.cos(angle) + np.sin(angle)
        else:
            angle = 2 * np.pi * ((n2[:, None] * (j + XP * k2[None, :])) % W) / W
            cos, sin = np.cos(angle), np.sin(angle)
            table[j] = np.block([[cos, -sin], [sin, cos]])
    return table


def x_frequencies():
    k2 = np.arange(XQ)
    result = np.zeros((NJ, 2 * XQ))
    for j in range(NJ):
        first, second = (0, 12) if j == 0 else (j, j)
        for half, k1 in enumerate((first, second)):
            k = k1 + XP * k2
            result[j, half * XQ : (half + 1) * XQ] = np.where(2 * k < W, k, k - W) / W
    return result


def y_frequencies():
    a = np.arange(YB)
    return np.where(2 * a < YB, a, a - YB) / YB


def y_tables():
    y = np.arange(HALF)
    wanted = np.array(
        [
            ROWS * d + first + i
            for first, count in PARTS
            for d in range(TILTS // 2)
            for i in range(count)
        ]
    )
    left, right = [], []
    for odd in range(2):
        a = np.arange(odd, YB, 2)

        def cas(rows):
            angle = 2 * np.pi * ((rows[:, None] * a[None, :]) % YB) / YB
            return np.cos(angle) + np.sin(angle)

        left.append(cas(wanted) / YB)
        given = cas(y).T
        swapped = np.concatenate([given[:, QUARTER:], given[:, :QUARTER]], axis=1)
        right.append([given, swapped])
    return np.array(left, np.float32), np.array(right, np.float32)


def real_eight(x):
    s0, d0 = x[0] + x[4], x[0] - x[4]
    s1, d1 = x[1] + x[5], x[1] - x[5]
    s2, d2 = x[2] + x[6], x[2] - x[6]
    s3, d3 = x[3] + x[7], x[3] - x[7]
    t0, t1 = s0 + s2, s1 + s3
    u = (d1 - d3) * root_half
    v = (d1 + d3) * root_half
    return {
        0: (t0 + t1, None),
        4: (t0 - t1, None),
        2: (s0 - s2, s3 - s1),
        1: (d0 + u, -(d2 + v)),
        3: (d0 - u, d2 - v),
    }


def forward_24(x):
    parts = [real_eight([x[(8 * a + 3 * b) % 24] for b in range(8)]) for a in range(3)]
    found = {}

    def put(ka, kb, value):
        for k in range(24):
            if k % 3 == ka % 3 and k % 8 == kb % 8:
                if k <= 12:
                    found[k] = value
                else:
                    re, im = value
                    found[24 - k] = (re, None if im is None else -im)

    for kb in (0, 4):
        p, q, r = (parts[a][kb][0] for a in range(3))
        total = q + r
        put(0, kb, (p + total, None))
        put(1, kb, (p - 0.5 * total, (r - q) * sin_third))
    for kb in (1, 2, 3):
        (pr, pi), (qr, qi), (rr, ri) = (parts[a][kb] for a in range(3))
        tr, ti = qr + rr, qi + ri
        put(0, kb, (pr + tr, pi + ti))
        mr, mi = pr - 0.5 * tr, pi - 0.5 * ti
        er, ei = (qr - rr) * sin_third, (qi - ri) * sin_third
        put(1, kb, (mr + ei, mi - er))
        put(2, kb, (mr - ei, mi + er))
    return found


def inverse_24(v):
    def get(ka, kb):
        k = next(i for i in range(24) if i % 3 == ka and i % 8 == kb)
        if k <= 12:
            return v[k]
        re, im = v[24 - k]
        return (re, -im)

    eights = [dict() for _ in range(3)]
    for kb in (0, 4):
        p = get(0, kb)[0]
        sr, si = get(1, kb)
        m = p - 0.5 * sr
        e = si * sin_third
        eights[0][kb] = (p + sr, None)
        eights[1][kb] = (m - e, None)
        eights[2][kb] = (m + e, None)
    for kb in (1, 2, 3):
        (pr, pi), (qr, qi), (rr, ri) = get(0, kb), get(1, kb), get(2, kb)
        tr, ti = qr + rr, qi + ri
        mr, mi = pr - 0.5 * tr, pi - 0.5 * ti
        er, ei = (qr - rr) * sin_third, (qi - ri) * sin_third
        eights[0][kb] = (pr + tr, pi + ti)
        eights[1][kb] = (mr - ei, mi + er)
        eights[2][kb] = (mr + ei, mi - er)
    out = [None] * 24
    for a in range(3):
        g = eights[a]
        g0, g4 = g[0][0], g[4][0]
        (r1, i1), (r2, i2), (r3, i3) = g[1], g[2], g[3]
        c0, c1 = g0 + g4, g0 - g4
        e0, e2 = c0 + r2, c0 - r2
        o0, o2 = r1 + r3, i1 - i3
        e1, e3 = c1 - i2, c1 + i2
        da, db = (r1 - r3) * root_half, (i1 + i3) * root_half
        o1, o3 = da - db, -(da + db)
        values = [e0 + o0, e1 + o1, e2 - o2, e3 + o3, e0 - o0, e1 - o1, e2 + o2, e3 - o3]
        for b in range(8):
            out[(8 * a + 3 * b) % 24] = values[b]
    return out


def split(value):
    high = value.astype(jnp.bfloat16)
    low = (value - high.astype(jnp.float32)).astype(jnp.bfloat16)
    return high, low


def three_products(high, low, table_high, table_low):
    left = jnp.concatenate([high, low, high], axis=1)
    right = jnp.concatenate([table_high, table_high, table_low], axis=0)
    return jnp.dot(left, right, preferred_element_type=jnp.float32)


STRIP = 16


def load_strips(x_refs, vh, vl, place=0):
    for n, x_ref in enumerate(x_refs, place):

        def strip(i, carry):
            rows = pl.ds(pl.multiple_of(i * STRIP, STRIP), STRIP)
            target = pl.ds(pl.multiple_of(n * QUARTER + i * STRIP, STRIP), STRIP)
            blocks = [
                x_ref[rows, b * XQ : (b + 1) * XQ].astype(jnp.float32) for b in range(XP)
            ]
            found = forward_24(blocks)
            for jj in range(NJ):
                if jj == 0:
                    pair = (found[0][0], found[12][0])
                else:
                    pair = found[jj]
                for half in range(2):
                    high, low = split(pair[half])
                    vh[jj, target, half * XQ : (half + 1) * XQ] = high
                    vl[jj, target, half * XQ : (half + 1) * XQ] = low
            return carry

        lax.fori_loop(0, QUARTER // STRIP, strip, 0, unroll=2)


def near_kernel(focus_ref, slab_ref, xa_ref, xb_ref, fh, fl, left_ref, right_ref, fy_ref, fx_ref,
                out_ref, mix_ref, gain_ref, vh, vl):
    load_strips((xa_ref, xb_ref), vh, vl)
    for j in range(NJ):
        out_ref[j] = three_products(vh[j], vl[j], fh[j], fl[j])
    scale = chi_scale * focus_ref[0]
    slab = slab_ref[0]
    angle_x = scale * (fx_ref[...] * fx_ref[...])
    cos_x, sin_x = jnp.cos(angle_x), jnp.sin(angle_x)
    for j in range(NJ):
        scaled = jnp.concatenate([cos_x[j : j + 1], sin_x[j : j + 1]], axis=0)
        gain_ref[j] = scaled * ((1.0 if j == 0 else 2.0) / W)
    for odd in range(2):
        fy = fy_ref[odd : odd + 1, :]
        angle_y = scale * (fy * fy) + phase_shift
        left = left_ref[odd]
        side = jnp.concatenate([left * -jnp.sin(angle_y), left * -jnp.cos(angle_y)], axis=0)
        right = right_ref[odd, slab & 1]
        mixed = jnp.dot(
            side, right, precision=lax.Precision.HIGHEST, preferred_element_type=jnp.float32
        )
        if odd:
            mixed = mixed * jnp.where(slab < 2, 1.0, -1.0)
        empty = jnp.zeros((YB, DEPTH - HALF), jnp.float32)
        high, low = split(jnp.concatenate([mixed, empty], axis=1))
        mix_ref[odd] = jnp.concatenate([high, low, high], axis=1)


def parameters(megabytes):
    return pltpu.CompilerParams(vmem_limit_bytes=megabytes * 2**20)


def scalar_spec():
    return pl.BlockSpec(memory_space=pltpu.SMEM)


def vmem_spec():
    return pl.BlockSpec(memory_space=pltpu.VMEM)


def run_near(focus, slab, xa, xb, fh, fl):
    left, right = y_tables()
    fy = y_frequencies()
    fy = np.stack([fy[0::2], fy[1::2]]).astype(np.float32)
    fx = x_frequencies().astype(np.float32)
    return pl.pallas_call(
        near_kernel,
        in_specs=[scalar_spec()] * 2 + [vmem_spec()] * 8,
        out_specs=[vmem_spec()] * 3,
        out_shape=[
            jax.ShapeDtypeStruct((NJ, HALF, 2 * XQ), jnp.float32),
            jax.ShapeDtypeStruct((2, YB, 3 * DEPTH), jnp.bfloat16),
            jax.ShapeDtypeStruct((NJ, 2, 2 * XQ), jnp.float32),
        ],
        scratch_shapes=[pltpu.VMEM((NJ, HALF, 2 * XQ), jnp.bfloat16)] * 2,
        compiler_params=parameters(NEAR_MB),
        name="near",
    )(focus, slab, xa, xb, fh, fl, *(jnp.asarray(t) for t in (left, right, fy, fx)))


NEAR_MB = 24
MAIN_MB = 40
PROJECT_MB = 24


def quarter_kernel(x_ref, fh, fl, out_ref, vh, vl):
    load_strips((x_ref,), vh, vl)
    for j in range(NJ):
        out_ref[j] = three_products(vh[j], vl[j], fh[j], fl[j])


def run_quarter(x, fh, fl):
    return pl.pallas_call(
        quarter_kernel,
        in_specs=[vmem_spec()] * 3,
        out_specs=vmem_spec(),
        out_shape=jax.ShapeDtypeStruct((NJ, QUARTER, 2 * XQ), jnp.float32),
        scratch_shapes=[pltpu.VMEM((NJ, QUARTER, 2 * XQ), jnp.bfloat16)] * 2,
        compiler_params=parameters(NEAR_MB),
        name="quarter",
    )(x, fh, fl)


def main_kernel(xb, near, quarter, mix, gain, fh, fl, out, vh, vl, eh, el, oh, ol, zh, zl, back):
    load_strips((xb,), vh, vl)
    for j in range(NJ):
        last = three_products(vh[j], vl[j], fh[j], fl[j])
        far = jnp.concatenate([quarter[j], last], axis=0)
        here = near[j]
        eh[j], el[j] = split(here + far)
        oh[j], ol[j] = split(here - far)
    empty = jnp.zeros((DEPTH - HALF, 2 * XQ), jnp.bfloat16)
    for j in range(NJ):
        factors = gain[j]

        def mixed(odd, high, low):
            right = jnp.concatenate([high, empty, high, empty, low, empty], axis=0)
            y = jnp.dot(mix[odd], right, preferred_element_type=jnp.float32)
            return y[:HALF] * factors[0:1] + y[HALF:] * factors[1:2]

        even, odd = mixed(0, eh[j], el[j]), mixed(1, oh[j], ol[j])
        zh[j], zl[j] = split(jnp.concatenate([even + odd, even - odd], axis=0))
    for j in range(NJ):
        left = jnp.concatenate([zh[j], zl[j], zh[j]], axis=1)
        right = jnp.concatenate([fh[j], fh[j], fl[j]], axis=1)
        back[j] = lax.dot_general(
            left, right, (((1,), (1,)), ((), ())), preferred_element_type=jnp.float32
        )

    devices = TILTS // 2
    for half in range(2):
        low_row, low_tile = half * HALF, 0
        for _, count in PARTS:
            per_strip, per_tile = 8 // count, 16 // count

            def strip(i, carry):
                cut = pl.ds(pl.multiple_of(low_row + i * 8, 8), 8)
                v = {}
                for jj in range(NJ):
                    one, two = back[jj, cut, 0:XQ], back[jj, cut, XQ : 2 * XQ]
                    if jj == 0:
                        v[0], v[12] = (one, None), (two, None)
                    else:
                        v[jj] = (one, two)
                values = inverse_24(v)
                for part in range(per_strip):
                    some = slice(part * count, (part + 1) * count)
                    place = half * devices + i * per_strip + part
                    for tile in range(XP // per_tile):
                        joined = jnp.concatenate(
                            [values[per_tile * tile + n][some] for n in range(per_tile)], axis=0
                        )
                        out[place, low_tile + tile] = joined.astype(jnp.bfloat16)
                return carry

            lax.fori_loop(0, devices // per_strip, strip, 0, unroll=8)
            low_row += devices * count
            low_tile += XP // per_tile


def run_main(xb, near, quarter, mix, gain, fh, fl):
    args = (xb, near, quarter, mix, gain, fh, fl)
    fourth = pltpu.VMEM((NJ, QUARTER, 2 * XQ), jnp.bfloat16)
    half = pltpu.VMEM((NJ, HALF, 2 * XQ), jnp.bfloat16)
    full = pltpu.VMEM((NJ, YB, 2 * XQ), jnp.bfloat16)
    return pl.pallas_call(
        main_kernel,
        in_specs=[vmem_spec()] * len(args),
        out_specs=vmem_spec(),
        out_shape=jax.ShapeDtypeStruct((TILTS, TILES, 16, XQ), jnp.bfloat16),
        scratch_shapes=[fourth] * 2 + [half] * 4 + [full] * 2 + [pltpu.VMEM((NJ, YB, 2 * XQ), jnp.float32)],
        compiler_params=parameters(MAIN_MB),
        name="main",
    )(*args)


def project_kernel(off_ref, weight_ref, x, out_ref, wide, narrow, total):
    wide[...] = jnp.zeros_like(wide)
    narrow[...] = jnp.zeros_like(narrow)
    total[...] = jnp.zeros_like(total)
    layouts = []
    base = 0
    for padded, (_, count) in zip((wide, narrow), PARTS):
        per_tile = 16 // count
        layouts.append((padded, count, per_tile, XP // per_tile, base))
        base += XP // per_tile

    def window(g, start):
        pieces = []
        for padded, count, per_tile, tiles, _ in layouts:
            log_tile = per_tile.bit_length() - 1
            piece = padded[start & (per_tile - 1), g, pl.ds(start >> log_tile, tiles)]
            pieces.append(piece.reshape(tiles * 16, XQ))
        return jnp.concatenate(pieces, axis=0)

    distance = lax.broadcasted_iota(jnp.int32, (2 * XQ, XQ), 0) - lax.broadcasted_iota(
        jnp.int32, (2 * XQ, XQ), 1
    )
    distance = distance.astype(jnp.int16)

    def band_of(t, z):
        shift = off_ref[t, z] & (XQ - 1)
        band = jnp.zeros((2 * XQ, XQ), jnp.bfloat16)
        for tap in range(TAPS):
            weight = weight_ref[t, z * TAPS + tap].astype(jnp.bfloat16)
            band = jnp.where(distance == (shift + tap).astype(jnp.int16), weight, band)
        return band

    def step(i, carry):
        late = 0
        for g in range(GROUP):
            t = i * GROUP + g
            for z in range(ZD):
                late += jnp.where((off_ref[t, z] & (XQ - 1)) > XQ - TAPS + 1, 1, 0)
            for padded, count, per_tile, tiles, base in layouts:
                lead = LEFT // per_tile
                rows = [x[t, base + p].astype(jnp.float32) for p in range(tiles)]
                empty = jnp.zeros((16, XQ), jnp.float32)
                for p in range(tiles):
                    padded[0, g, lead + p] = x[t, base + p]
                for m in range(1, per_tile):
                    for p in range(-1, tiles):
                        here = rows[p] if p >= 0 else empty
                        later = rows[p + 1] if p + 1 < tiles else empty
                        tile = jnp.concatenate([here[m * count :], later[: m * count]], axis=0)
                        padded[m, g, lead + p] = tile.astype(jnp.bfloat16)
        for z in range(ZD):
            parts = []
            for g in range(GROUP):
                start = (off_ref[i * GROUP + g, z] >> 7) + LEFT
                parts.append(window(g, start))
                parts.append(window(g, start + 1))
            left = jnp.concatenate(parts, axis=1)
            band = jnp.concatenate([band_of(i * GROUP + g, z) for g in range(GROUP)], axis=0)
            total[z] += jnp.dot(left, band, preferred_element_type=jnp.float32)

        @pl.when(late > 0)
        def _():
            def pair(n, carry):
                g, z = n // ZD, n % ZD
                t = i * GROUP + g
                shift = off_ref[t, z] & (XQ - 1)

                @pl.when(shift > XQ - TAPS + 1)
                def _():
                    moved = (
                        lax.broadcasted_iota(jnp.int32, (XQ, XQ), 0)
                        - lax.broadcasted_iota(jnp.int32, (XQ, XQ), 1)
                        + (2 * XQ - shift)
                    )
                    band = jnp.zeros((XQ, XQ), jnp.float32)
                    for tap in range(TAPS):
                        band = jnp.where(moved == tap, weight_ref[t, z * TAPS + tap], band)
                    start = (off_ref[t, z] >> 7) + LEFT
                    total[z] += jnp.dot(
                        window(g, start + 2),
                        band.astype(jnp.bfloat16),
                        preferred_element_type=jnp.float32,
                    )

                return carry

            lax.fori_loop(0, GROUP * ZD, pair, 0)

        return carry

    lax.fori_loop(0, TILTS // GROUP, step, 0)
    for z in range(ZD):
        for (first, count), (_, _, _, _, base) in zip(PARTS, layouts):
            for b in range(XP):
                row = base * 16 + b * count
                out_ref[first : first + count, z, b * XQ : (b + 1) * XQ] = total[
                    z, row : row + count, :
                ]


def run_project(off, weights, moved):
    return pl.pallas_call(
        project_kernel,
        in_specs=[scalar_spec()] * 2 + [vmem_spec()],
        out_specs=vmem_spec(),
        out_shape=jax.ShapeDtypeStruct((ROWS, ZD, W), jnp.float32),
        scratch_shapes=[
            pltpu.VMEM((2, GROUP, SPAN // 2, 16, XQ), jnp.bfloat16),
            pltpu.VMEM((4, GROUP, SPAN // 4, 16, XQ), jnp.bfloat16),
            pltpu.VMEM((ZD, TILES * 16, XQ), jnp.float32),
        ],
        compiler_params=parameters(PROJECT_MB),
        name="project",
    )(off, weights, moved)


def body(tilts, tilt_defocus, defocus_table, slab_pick, interp_offset, interp_weights):
    def swap(block, bit):
        return lax.ppermute(block, "slab", [(i, i ^ bit) for i in range(4)])

    own = tilts[0]
    beside = swap(own, 1)
    across = swap(own, 2)
    entries = jnp.arange(defocus_table.shape[0], dtype=jnp.int32)
    group_defocus = jnp.sum(jnp.where(entries == slab_pick[0], defocus_table, 0.0))
    focus = tilt_defocus + group_defocus
    slab = lax.axis_index("slab").astype(jnp.int32).reshape(1)
    fh, fl = (jnp.asarray(t) for t in split_np(x_table()))
    near, mix, gain = run_near(focus, slab, own, beside, fh, fl)
    near, across = lax.optimization_barrier((near, across))
    opposite = swap(across, 1)
    weights = interp_weights.astype(jnp.float32).reshape(TILTS, ZD * TAPS)
    quarter = run_quarter(across, fh, fl)
    quarter, opposite = lax.optimization_barrier((quarter, opposite))
    filtered = run_main(opposite, near, quarter, mix, gain, fh, fl)
    moved = lax.all_to_all(filtered, "dev", split_axis=0, concat_axis=0, tiled=True)
    return run_project(interp_offset, weights, moved)


def solution(mesh):
    in_specs = (
        P("dev", "slab", None),
        P("dev"),
        P(),
        P("slab"),
        P(None, "slab"),
        P(None, "slab", None),
    )
    out_specs = P("dev", "slab", None)
    return jax.shard_map(body, mesh=mesh, in_specs=in_specs, out_specs=out_specs, check_vma=False)
```
